128 devices in a mesh: hold: 16 (over y, x_hi, core), bulk: 8 (over z, x_lo).
Axes of the slice: x: 4 (x_hi: 2, x_lo: 2; x = x_hi * 2 + x_lo), y: 4, z: 4, core: 2. Of those that a mesh axis runs over, the one named last changes fastest.
Arguments:
- queries: bfloat16 [2048, 8192], P(('hold', 'bulk')), may hold values from -12 to 12
- out_grad: bfloat16 [2048, 8192], P(('hold', 'bulk')), may hold values from -48 to 48
- attn_out: bfloat16 [2048, 8192], P(('hold', 'bulk')), may hold values from -3 to 3
- log_totals: float32 [2048, 64], P('hold', 'bulk'), may hold values from 11 to 13
- prompt_keys: bfloat16 [16384, 1024], P('hold', 'bulk'), may hold values from -6 to 6
- prompt_values: bfloat16 [16384, 1024], P('hold', 'bulk'), may hold values from -6 to 6
- rollout_keys: bfloat16 [2048, 1024], P('hold', 'bulk'), may hold values from -6 to 6
- rollout_values: bfloat16 [2048, 1024], P('hold', 'bulk'), may hold values from -6 to 6
- rollout_blocks: int32 [8], replicated, may hold values from 1 to 4, 16 in all
Outputs:
- query_grad: bfloat16 [2048, 8192], P(('hold', 'bulk'))
- prompt_key_grad: float32 [16384, 1024], P('hold', 'bulk')
- prompt_value_grad: float32 [16384, 1024], P('hold', 'bulk')
- rollout_key_grad: float32 [2048, 1024], P('hold', 'bulk')
- rollout_value_grad: float32 [2048, 1024], P('hold', 'bulk')
The draws below stay inside these ranges and needn't reach their ends.
Inputs may be any that keep to these rules, and one draw needn't show every extreme that they name: `rollout_blocks`: the entries sum to 16; the largest is exactly 4.
All inputs are finite; a program needn't handle non-finite values.
Results may differ from the reference program's by a relative error of at most 0.0055.
Values may be sent and summed in bfloat16 or wider, within the bound.
No kernel may reach another device: no remote copies, remote signals or barrier semaphores. Data moves between devices by JAX's collectives and lax.ppermute only.
A program may use at most 128 MiB of HBM per device.

```python
import math
import jax
import jax.numpy as jnp
import numpy as np
from jax import lax

HD = 128
GROUP = 8
BLOCK = 128
KV_HEADS = 8
HEADS = 64
PROMPT = 16384
ROWS = 2048
NROLL = 8
TOTAL_BLOCKS = 16
MOST_BLOCKS = 4


def shard_levels(rng, extent, cuts, low, high):
    factor_of, own = 1.0, jax.random.fold_in(rng, 6)
    for axis_at, shards_of in cuts:
        draws = jnp.exp(jax.random.uniform(jax.random.fold_in(own, axis_at), (shards_of,), jnp.float32, low / len(cuts), high / len(cuts)))
        factor_of = factor_of * jnp.repeat(draws, extent[axis_at] // shards_of).reshape([-1 if axis == axis_at else 1 for axis in range(len(extent))])
    return factor_of


def length_profile(amount, total, most, slope):
    portions = [(1 << 20) // math.isqrt(rank ** slope) + 1 for rank in range(2, amount + 1)]
    surplus, given = total - most - (amount - 1), [1] * (amount - 1)
    while surplus > 0:
        movable = [i for i in range(amount - 1) if given[i] < most]
        mass, remaining = sum([portions[i] for i in movable]), surplus
        for i in movable:
            more = min(most - given[i], max(1, remaining * portions[i] // mass), surplus)
            given[i] = given[i] + more
            surplus = surplus - more
    return np.array([most] + given)


def ragged_sizes(own_key, number_of, total, bound, lean):
    if number_of == 2:
        one = jax.random.randint(own_key, (), max(1, total - bound), min(bound, total - 1) + 1)
        return jnp.stack([one, total - one])
    sizes = jnp.asarray(length_profile(number_of, total, bound, lean), jnp.int32)
    couples = (number_of - 1) // 2
    source_of, sink = sizes[1:1 + 2 * couples:2], sizes[2:2 + 2 * couples:2]
    room = jnp.minimum(source_of - 1, bound - sink)
    shifted = jax.random.randint(jax.random.fold_in(own_key, 1), (couples,), 0, 1 << 20) % (room + 1)
    sizes = sizes.at[1:1 + 2 * couples:2].set(source_of - shifted).at[2:2 + 2 * couples:2].set(sink + shifted)
    return sizes[jax.random.permutation(jax.random.fold_in(own_key, 2), number_of)]


def centred(own_key, dims, spread, limit, pieces=(), held_as=jnp.bfloat16):
    factor_of = shard_levels(own_key, dims, pieces, -0.22, 0.18) if pieces else 1.0
    array = jax.random.normal(own_key, dims, jnp.float32) * spread * factor_of
    return jnp.minimum(jnp.maximum(array, -limit), limit).astype(held_as)


def setup_inputs(seed: int = 0) -> dict:
    key_of = jax.random.split(jax.random.key(seed), 10)
    queries = centred(key_of[0], (ROWS, HEADS * HD), 2.0, 12.0, ((0, 128),))
    out_grad = centred(key_of[1], (ROWS, HEADS * HD), 8.0, 48.0, ((0, 128),))
    attn_out = centred(key_of[2], (ROWS, HEADS * HD), 0.5, 3.0, ((0, 128),))
    log_totals = jnp.clip(11.0 + 2.0 * jax.random.uniform(key_of[3], (ROWS, HEADS), jnp.float32) ** shard_levels(key_of[3], (ROWS, HEADS), ((0, 16), (1, 8)), -0.2, 0.2), 11.0, 13.0)
    prompt_keys = centred(key_of[4], (PROMPT, KV_HEADS * HD), 1.0, 6.0, ((0, 16), (1, 8)))
    prompt_values = centred(key_of[5], (PROMPT, KV_HEADS * HD), 1.0, 6.0, ((0, 16), (1, 8)))
    rollout_keys = centred(key_of[6], (ROWS, KV_HEADS * HD), 1.0, 6.0, ((0, 16), (1, 8)))
    rollout_values = centred(key_of[7], (ROWS, KV_HEADS * HD), 1.0, 6.0, ((0, 16), (1, 8)))
    rollout_blocks = ragged_sizes(key_of[8], NROLL, TOTAL_BLOCKS, MOST_BLOCKS, 2).astype(jnp.int32)
    return {"queries": queries, "out_grad": out_grad, "attn_out": attn_out, "log_totals": log_totals, "prompt_keys": prompt_keys, "prompt_values": prompt_values, "rollout_keys": rollout_keys, "rollout_values": rollout_values, "rollout_blocks": rollout_blocks}


def segment_of(positions, ends):
    return jnp.sum((positions[:, None] >= ends[None, :]).astype(jnp.int32), axis=1)


def head_grads(query, grad_out, log_total, offset_term, keys, values, ends):
    total = keys.shape[0]
    columns = jnp.arange(total, dtype=jnp.int32) - PROMPT
    key_prompt = columns < 0
    key_seg = segment_of(jnp.maximum(columns, 0), ends)
    scale = HD ** -0.5
    width = math.gcd(ROWS, 256)
    blocks = ROWS // width
    row_ids = jnp.arange(ROWS, dtype=jnp.int32).reshape(blocks, width)
    high = lax.Precision.HIGHEST

    def step(carry, items):
        key_acc, value_acc = carry
        block_query, block_grad, block_log, block_offset, block_rows = items
        query_seg = segment_of(block_rows, ends)
        allowed = key_prompt[None, :] | ((query_seg[:, None] == key_seg[None, :]) & (columns[None, :] <= block_rows[:, None]))
        scores = jnp.einsum('ngd,md->ngm', block_query, keys, precision=high) * scale
        prob = jnp.where(allowed[:, None, :], jnp.exp(scores - block_log[:, :, None]), 0.0)
        prob_b = lax.optimization_barrier(prob.astype(jnp.bfloat16)).astype(jnp.float32)
        value_acc = value_acc + jnp.einsum('ngm,ngd->md', prob_b, block_grad, precision=high)
        dprob = jnp.einsum('ngd,md->ngm', block_grad, values, precision=high)
        dscore = lax.optimization_barrier((prob * (dprob - block_offset[:, :, None])).astype(jnp.bfloat16)).astype(jnp.float32)
        query_part = jnp.einsum('ngm,md->ngd', dscore, keys, precision=high) * scale
        key_acc = key_acc + jnp.einsum('ngm,ngd->md', dscore, block_query, precision=high) * scale
        return (key_acc, value_acc), query_part

    def split(arr):
        return arr.reshape((blocks, width) + arr.shape[1:])

    zeros = jnp.zeros((total, HD), jnp.float32)
    (key_grad, value_grad), query_grad = lax.scan(step, (zeros, zeros), (split(query), split(grad_out), split(log_total), split(offset_term), row_ids))
    return query_grad.reshape(ROWS, GROUP, HD), key_grad, value_grad


def reference(queries, out_grad, attn_out, log_totals, prompt_keys, prompt_values, rollout_keys, rollout_values, rollout_blocks):
    ends = jnp.cumsum(rollout_blocks).astype(jnp.int32) * BLOCK
    query = queries.astype(jnp.float32).reshape(ROWS, KV_HEADS, GROUP, HD)
    grad_out = out_grad.astype(jnp.float32).reshape(ROWS, KV_HEADS, GROUP, HD)
    outputs = attn_out.astype(jnp.float32).reshape(ROWS, KV_HEADS, GROUP, HD)
    offset_term = jnp.sum(grad_out * outputs, axis=-1)
    log_total = log_totals.reshape(ROWS, KV_HEADS, GROUP)
    keys = jnp.concatenate([prompt_keys, rollout_keys], 0).astype(jnp.float32).reshape(PROMPT + ROWS, KV_HEADS, HD)
    values = jnp.concatenate([prompt_values, rollout_values], 0).astype(jnp.float32).reshape(PROMPT + ROWS, KV_HEADS, HD)

    def per_head(items):
        head_query, head_grad, head_log, head_offset, head_keys, head_values = items
        return head_grads(head_query, head_grad, head_log, head_offset, head_keys, head_values, ends)

    query_grad, key_grad, value_grad = lax.map(per_head, (
        query.transpose(1, 0, 2, 3), grad_out.transpose(1, 0, 2, 3),
        log_total.transpose(1, 0, 2), offset_term.transpose(1, 0, 2),
        keys.transpose(1, 0, 2), values.transpose(1, 0, 2)))
    query_grad = query_grad.transpose(1, 0, 2, 3).reshape(ROWS, HEADS * HD).astype(jnp.bfloat16)
    key_grad = key_grad.transpose(1, 0, 2).reshape(PROMPT + ROWS, KV_HEADS * HD)
    value_grad = value_grad.transpose(1, 0, 2).reshape(PROMPT + ROWS, KV_HEADS * HD)
    return (query_grad, key_grad[:PROMPT], value_grad[:PROMPT], key_grad[PROMPT:], value_grad[PROMPT:])
```

```python
import functools

import jax
import jax.numpy as jnp
from jax import lax
from jax.experimental import pallas as pl
from jax.experimental.pallas import tpu as pltpu
from jax.sharding import Mesh
from jax.sharding import PartitionSpec as P

F32 = jnp.float32
BF16 = jnp.bfloat16
HD = 128
GROUP = 8
BLOCK = 128
NBLK = 16
PK = 1024
RK = 128
KW = PK + RK
QR = BLOCK * GROUP
SRC = 8
SUB = BLOCK // SRC
PAY = 2 * BLOCK + 16
SCALE = HD ** (-0.5)
LOG2E = 1.4426950408889634
C2 = SCALE * LOG2E

NN = (((1,), (0,)), ((), ()))
NT = (((1,), (1,)), ((), ()))

Y, XH, C, Z, XL = "y", "xh", "c", "z", "xl"
BULK = (Z, XL)


def dot(a, b, dims):
    return lax.dot_general(a, b, dims, preferred_element_type=F32)


def pack_kernel(q, g, o, pk, rk, pv, rv, pay, kv, sems):
    copies, at = [], 0
    for n, (src, rows) in enumerate(((pk, PK), (rk, RK), (pv, PK), (rv, RK))):
        copies.append(pltpu.make_async_copy(src, kv.at[pl.ds(at, rows)], sems.at[n]))
        at += rows
    for copy in copies:
        copy.start()
    ones = jnp.ones((16, HD), BF16)
    row = lax.broadcasted_iota(jnp.int32, (16, BLOCK), 0)
    for b in range(SRC):
        prods = []
        for h in range(GROUP):
            cols = slice((b * GROUP + h) * HD, (b * GROUP + h + 1) * HD)
            qh, gh = q[:, cols], g[:, cols]
            pay[b, h * SUB : (h + 1) * SUB, :] = qh
            pay[b, BLOCK + h * SUB : BLOCK + (h + 1) * SUB, :] = gh
            prods.append(gh.astype(F32) * o[:, cols].astype(F32))
        prod = jnp.concatenate(prods, axis=0)
        high = prod.astype(BF16)
        low = (prod - high.astype(F32)).astype(BF16)
        delta = dot(ones, high, NT) + dot(ones, low, NT)
        d1 = delta.astype(BF16).astype(F32)
        d2 = (delta - d1).astype(BF16).astype(F32)
        d3 = delta - d1 - d2
        pieces = jnp.where(row == 0, d1, jnp.where(row == 1, d2, jnp.where(row == 2, d3, 0.0)))
        pay[b, 2 * BLOCK : PAY, :] = pieces.astype(BF16)
    for copy in copies:
        copy.wait()


def pack(q, g, o, pk, rk, pv, rv):
    anyspec = pl.BlockSpec(memory_space=pl.ANY)
    vspec = pl.BlockSpec(memory_space=pltpu.VMEM)
    return pl.pallas_call(
        pack_kernel,
        in_specs=[vspec] * 3 + [anyspec] * 4,
        out_specs=[vspec, anyspec],
        out_shape=[
            jax.ShapeDtypeStruct((SRC, PAY, HD), BF16),
            jax.ShapeDtypeStruct((2 * KW, HD), BF16),
        ],
        scratch_shapes=[pltpu.SemaphoreType.DMA((4,))],
        compiler_params=pltpu.CompilerParams(vmem_limit_bytes=16 << 20),
        name="pack",
    )(q, g, o, pk, rk, pv, rv)


def row_vector(rows):
    return jnp.concatenate([rows[s : s + 1, :] for s in range(SRC)], axis=1)


def column(rows):
    return jnp.broadcast_to(row_vector(rows), (HD, QR)).T


def tiles_kernel(cfg, *refs):
    unit, keys_of, kv_in, dq_in, final = cfg
    nk = len(keys_of)
    refs = list(refs)

    def take(n):
        out = refs[:n]
        del refs[:n]
        return out

    place, lengths, logs = take(3)
    pay_in = take(1 if unit == "own" else 2)
    dq_src = take(1) if dq_in else []
    key_in = take(nk)
    kv_src = dict(zip([n for n in range(nk) if kv_in[n]], take(sum(kv_in))))
    halves = final and unit in ("near_a", "near_b")
    dq_out = take(2 if halves else 1)
    kv_out = take(nk)
    pay, keys, acc, dqa, sem_q, sem_k, sem_a, sem_o = refs

    loads = []
    if unit == "own":
        loads.append(pltpu.make_async_copy(pay_in[0], pay, sem_q.at[0]))
    else:
        for h in range(2):
            loads.append(pltpu.make_async_copy(pay_in[h], pay.at[pl.ds(4 * h, 4)], sem_q.at[h]))
    if dq_in:
        loads.append(pltpu.make_async_copy(dq_src[0], dqa, sem_q.at[2]))
    for copy in loads:
        copy.start()
    for n in range(nk):
        pltpu.make_async_copy(key_in[n], keys.at[n], sem_k.at[n]).start()
        if kv_in[n]:
            pltpu.make_async_copy(kv_src[n], acc.at[n], sem_a.at[n]).start()
        else:
            acc[n] = jnp.zeros((2 * HD, KW), F32)
    if not dq_in:
        dqa[...] = jnp.zeros((QR, HD), F32)

    y, xh, c = place[0], place[1], place[2]
    if unit == "own":
        log_rows = logs[0] if logs.shape[0] == 1 else logs[y]
    elif unit == "opp":
        log_rows = logs[(y + 2) % 4]
    else:
        up, down = logs[(y + 1) % 4], logs[(y + 3) % 4]
        parts = [up[0:4], down[4:8]] if unit == "near_a" else [up[4:8], down[0:4]]
        log_rows = jnp.concatenate(parts, axis=0)
    log_col = column(log_rows)
    for copy in loads:
        copy.wait()
    pieces = pay[:, 2 * BLOCK : PAY, :].astype(F32)
    delta_col = column(pieces[:, 0, :] + pieces[:, 1, :] + pieces[:, 2, :])
    q = pay[:, 0:BLOCK, :].reshape(QR, HD)
    g = pay[:, BLOCK : 2 * BLOCK, :].reshape(QR, HD)
    qt, gt = q.T, g.T

    def step(j, carry):
        pltpu.make_async_copy(key_in[0], keys.at[j], sem_k.at[j]).wait()
        for n in range(nk):
            if kv_in[n]:

                @pl.when(j == n)
                def _():
                    pltpu.make_async_copy(kv_src[n], acc.at[n], sem_a.at[n]).wait()

        def products(at, width, rows):
            s = dot(q[:rows], keys[j, at : at + width, :], NT)
            dp = dot(g[:rows], keys[j, KW + at : KW + at + width, :], NT)
            return s, dp

        def grads(at, width, rows, s, dp, allowed):
            wide = lambda col: jnp.concatenate([col[:rows]] * (width // HD), axis=1)
            p = jnp.exp2(s * C2 - wide(log_col))
            if allowed is not None:
                p = jnp.where(allowed, p, 0.0)
            ds = (p * (dp - wide(delta_col))).astype(BF16)
            p = p.astype(BF16)
            acc[j, 0:HD, at : at + width] += dot(qt[:, :rows], ds, NN)
            acc[j, HD : 2 * HD, at : at + width] += dot(gt[:, :rows], p, NN)
            return dot(ds, keys[j, at : at + width, :], NN)

        part = 256
        total = None
        ahead = products(0, part, QR)
        for n in range(PK // part):
            s, dp = ahead
            if n + 1 < PK // part:
                ahead = products((n + 1) * part, part, QR)
            term = grads(n * part, part, QR, s, dp, None)
            total = term if total is None else total + term
        dqa[...] += total

        if unit != "opp":
            rows = QR if unit == "own" else QR // 2
            qi = 4 * (y if unit == "own" else (y + 1) % 4) + 2 * xh + c
            fx = sum(jnp.where(j == n, keys_of[n][0], 0) for n in range(nk))
            fc = sum(jnp.where(j == n, keys_of[n][1], 0) for n in range(nk))
            kj = 4 * y + 2 * (xh + fx - 2 * xh * fx) + (c + fc - 2 * c * fc)
            seen, end = kj <= qi, 0
            for r in range(lengths.shape[0]):
                end = end + lengths[r]
                seen = seen & ((end <= kj) | (end > qi))

            @pl.when(seen)
            def _():
                allowed = None
                if unit == "own":
                    row = lax.broadcasted_iota(jnp.int32, (rows, RK), 0)
                    key_at = lax.broadcasted_iota(jnp.int32, (rows, RK), 1)
                    token = (row // BLOCK) * SUB + row % SUB
                    allowed = (kj < qi) | (key_at <= token)
                s, dp = products(PK, RK, rows)
                dqa[:rows, :] += grads(PK, RK, rows, s, dp, allowed)

        for n in range(nk):

            @pl.when(j == n)
            def _():
                pltpu.make_async_copy(acc.at[n], kv_out[n], sem_o.at[n]).start()

        return carry

    lax.fori_loop(0, nk, step, 0)
    if final and unit != "own":
        done = (dqa[...] * SCALE).astype(BF16).reshape(SRC, BLOCK, HD)
        if halves:
            dq_out[0][...], dq_out[1][...] = done[0:4], done[4:8]
        else:
            dq_out[0][...] = done
    else:
        dq_out[0][...] = dqa[...]
    for n in range(nk):
        pltpu.make_async_copy(acc.at[n], kv_out[n], sem_o.at[n]).wait()


def tiles(name, unit, common, pays, keys_of, keys, sums, dq=None, final=False):
    nk = len(keys)
    kv_in = tuple(g is not None for g in sums)
    cfg = (unit, tuple(keys_of), kv_in, dq is not None, final)
    anyspec = pl.BlockSpec(memory_space=pl.ANY)
    vspec = pl.BlockSpec(memory_space=pltpu.VMEM)
    sspec = pl.BlockSpec(memory_space=pltpu.SMEM)
    operands = list(common) + list(pays) + ([dq] if dq is not None else []) + list(keys)
    specs = [sspec, sspec, vspec] + [anyspec] * (len(operands) - 3)
    if not final or unit == "own":
        dq_shapes = [jax.ShapeDtypeStruct((QR, HD), F32)]
    elif unit == "opp":
        dq_shapes = [jax.ShapeDtypeStruct((SRC, BLOCK, HD), BF16)]
    else:
        dq_shapes = [jax.ShapeDtypeStruct((SRC // 2, BLOCK, HD), BF16)] * 2
    aliases = {}
    for n in range(nk):
        if kv_in[n]:
            aliases[len(operands)] = len(dq_shapes) + n
            operands.append(sums[n])
            specs.append(anyspec)
    outs = pl.pallas_call(
        functools.partial(tiles_kernel, cfg),
        in_specs=specs,
        out_specs=[vspec] * len(dq_shapes) + [anyspec] * nk,
        out_shape=dq_shapes + [jax.ShapeDtypeStruct((2 * HD, KW), F32)] * nk,
        scratch_shapes=[
            pltpu.VMEM((SRC, PAY, HD), BF16),
            pltpu.VMEM((nk, 2 * KW, HD), BF16),
            pltpu.VMEM((nk, 2 * HD, KW), F32),
            pltpu.VMEM((QR, HD), F32),
            pltpu.SemaphoreType.DMA((3,)),
            pltpu.SemaphoreType.DMA((nk,)),
            pltpu.SemaphoreType.DMA((nk,)),
            pltpu.SemaphoreType.DMA((nk,)),
        ],
        input_output_aliases=aliases,
        compiler_params=pltpu.CompilerParams(vmem_limit_bytes=40 << 20),
        cost_estimate=pl.CostEstimate(
            flops=nk * 10 * QR * PK * HD, bytes_accessed=4 << 20, transcendentals=0
        ),
        name=name,
    )(*operands)
    dqs, sums = outs[: len(dq_shapes)], outs[len(dq_shapes) :]
    return (dqs[0] if len(dqs) == 1 else dqs), sums


def finish_kernel(own, up_a, up_b, down_a, down_b, opp, out):
    for s in range(SRC):
        up, down = (up_a, down_a) if s < 4 else (up_b, down_b)
        rows = own[s * BLOCK : (s + 1) * BLOCK, :] * SCALE
        rows = rows + up[s % 4].astype(F32) + down[s % 4].astype(F32) + opp[s].astype(F32)
        out[s] = rows.astype(BF16)


def finish(*terms):
    return pl.pallas_call(
        finish_kernel, out_shape=jax.ShapeDtypeStruct((SRC, BLOCK, HD), BF16), name="finish"
    )(*terms)


def close_kernel(own, core, chip, dk, dv, drk, drv):
    def total(rows, cols):
        part = own[rows, cols] + core[rows, cols] + chip[rows, cols].astype(F32)
        return part.T

    keys, values = slice(0, HD), slice(HD, 2 * HD)
    dk[...] = total(keys, slice(0, PK)) * SCALE
    drk[...] = total(keys, slice(PK, KW)) * SCALE
    dv[...] = total(values, slice(0, PK))
    drv[...] = total(values, slice(PK, KW))


def close(own, core, chip):
    shape = lambda rows: jax.ShapeDtypeStruct((rows, HD), F32)
    return pl.pallas_call(
        close_kernel, out_shape=[shape(PK), shape(PK), shape(RK), shape(RK)], name="close"
    )(own, core, chip)


def shift(n, s):
    return [(i, (i + s) % n) for i in range(n)]


def after(values, *earlier):
    return lax.optimization_barrier((values, earlier))[0]


def shards(
    queries,
    out_grad,
    attn_out,
    log_totals,
    prompt_keys,
    prompt_values,
    rollout_keys,
    rollout_values,
    rollout_blocks,
):
    place = jnp.stack([lax.axis_index(Y), lax.axis_index(XH), lax.axis_index(C)])
    place = place.astype(jnp.int32)
    to_next, to_last = shift(4, 1), shift(4, -1)
    swap = shift(2, 1)

    l0 = (log_totals * LOG2E).reshape(SRC, SUB, GROUP).transpose(0, 2, 1).reshape(SRC, BLOCK)
    l_all = lax.all_gather(l0, Y, axis=0, tiled=False)

    payload, kv_own = pack(
        queries, out_grad, attn_out, prompt_keys, rollout_keys, prompt_values, rollout_values
    )
    kv_x = lax.ppermute(kv_own, XH, swap)
    kv_c = lax.ppermute(kv_own, C, swap)
    kv_xc = lax.ppermute(kv_x, C, swap)
    own = lax.all_to_all(payload, BULK, split_axis=0, concat_axis=0, tiled=True)
    own_a, own_b = own[:4], own[4:]
    up_a = lax.ppermute(own_a, Y, to_last)
    down_b = lax.ppermute(own_b, Y, to_next)
    up_b = lax.ppermute(own_b, Y, to_last)
    down_a = lax.ppermute(own_a, Y, to_next)

    far, near = [(1, 0), (1, 1)], [(0, 0), (0, 1)]
    first, common = (place, rollout_blocks, l0[None]), (place, rollout_blocks, l_all)

    dq_own, (g_x, g_xc, g_c) = tiles(
        "own_3", "own", first, [own], far + near[1:], [kv_x, kv_xc, kv_c], [None] * 3
    )
    up_a, down_b = after((up_a, down_b), dq_own)
    opp_a = lax.ppermute(up_a, Y, to_last)
    opp_b = lax.ppermute(down_b, Y, to_next)
    dq_a, (g_x, g_xc) = tiles(
        "a_far", "near_a", common, [up_a, down_b], far, [kv_x, kv_xc], [g_x, g_xc]
    )
    up_b, down_a = after((up_b, down_a), dq_a)
    dq_b, (g_x, g_xc) = tiles(
        "b_far", "near_b", common, [up_b, down_a], far, [kv_x, kv_xc], [g_x, g_xc]
    )
    dq_a = after(dq_a, dq_b)
    (a_up, a_down), (g_own, g_c) = tiles(
        "a_near", "near_a", common, [up_a, down_b], near, [kv_own, kv_c], [None, g_c], dq_a, True
    )
    from_a_down = lax.ppermute(a_up, Y, to_next)
    from_a_up = lax.ppermute(a_down, Y, to_last)
    opp_a, opp_b = after((opp_a, opp_b), a_up)
    dq_opp, (g_x, g_xc) = tiles(
        "opp_far", "opp", common, [opp_a, opp_b], far, [kv_x, kv_xc], [g_x, g_xc]
    )
    from_core = lax.ppermute(g_xc, C, swap)
    opp, (g_own, g_c) = tiles(
        "opp_near", "opp", common, [opp_a, opp_b], near, [kv_own, kv_c], [g_own, g_c], dq_opp, True
    )
    from_opp = lax.ppermute(opp, Y, shift(4, 2))
    to_chip = (g_x + after(from_core, opp)).astype(BF16)
    from_chip = lax.ppermute(to_chip, XH, swap)
    dq_b = after(dq_b, to_chip)
    (b_up, b_down), (g_own, g_c) = tiles(
        "b_near", "near_b", common, [up_b, down_a], near, [kv_own, kv_c], [g_own, g_c], dq_b, True
    )
    from_b_down = lax.ppermute(b_up, Y, to_next)
    from_b_up = lax.ppermute(b_down, Y, to_last)
    from_c = lax.ppermute(g_c, C, swap)
    dq_own, (g_own,) = tiles(
        "own_1", "own", common, [own], near[:1], [kv_own], [g_own], dq_own, True
    )

    dq = finish(dq_own, from_b_up, from_a_up, from_a_down, from_b_down, from_opp)
    dq = lax.all_to_all(dq, BULK, split_axis=0, concat_axis=0, tiled=True)
    query_grad = dq.reshape(SRC * GROUP, SUB, HD).transpose(1, 0, 2).reshape(SUB, SRC * GROUP * HD)
    dk, dv, drk, drv = close(g_own, from_c, from_chip)
    return (query_grad, dk, dv, drk, drv)


def solution(mesh):
    fine = Mesh(mesh.devices.reshape(4, 2, 2, 4, 2), (Y, XH, C, Z, XL))
    hold, bulk = (Y, XH, C), (Z, XL)
    tokens = P(hold + bulk, None)
    split = P(hold, bulk)
    return jax.shard_map(
        shards,
        mesh=fine,
        in_specs=(tokens, tokens, tokens, split, split, split, split, split, P()),
        out_specs=(tokens, split, split, split, split),
        check_vma=False,
    )
```

```python
import functools

import jax
import jax.numpy as jnp
from jax import lax
from jax.experimental import pallas as pl
from jax.experimental.pallas import tpu as pltpu
from jax.sharding import Mesh
from jax.sharding import PartitionSpec as P

F32 = jnp.float32
BF16 = jnp.bfloat16
HD = 128
GROUP = 8
BLOCK = 128
NBLK = 16
PK = 1024
RK = 128
KW = PK + RK
QR = BLOCK * GROUP
SRC = 8
SUB = BLOCK // SRC
DROW = 2 * BLOCK
LROW = DROW + 8
PAY = LROW + 8
SCALE = HD ** (-0.5)
LOG2E = 1.4426950408889634
C2 = SCALE * LOG2E

NN = (((1,), (0,)), ((), ()))
NT = (((1,), (1,)), ((), ()))

Y, XH, C, Z, XL = "y", "xh", "c", "z", "xl"
BULK = (Z, XL)


def dot(a, b, dims):
    return lax.dot_general(a, b, dims, preferred_element_type=F32)


def held(*arrays):
    return [pltpu.with_memory_space_constraint(a, pltpu.VMEM) for a in arrays]


ANYSPEC = pl.BlockSpec(memory_space=pl.ANY)
VSPEC = pl.BlockSpec(memory_space=pltpu.VMEM)
SSPEC = pl.BlockSpec(memory_space=pltpu.SMEM)


def pieces_of(x):
    a = x.astype(BF16).astype(F32)
    b = (x - a).astype(BF16).astype(F32)
    return a, b, x - a - b


def pack_kernel(q_in, g_in, o_in, pk, rk, pv, rv, pay, kv, q, g, o, sems):
    loads = [
        pltpu.make_async_copy(src, dst, sems.at[n])
        for n, (src, dst) in enumerate(((q_in, q), (g_in, g), (o_in, o)))
    ]
    copies, at = [], 0
    for n, (src, rows) in enumerate(((pk, PK), (rk, RK), (pv, PK), (rv, RK))):
        copies.append(pltpu.make_async_copy(src, kv.at[pl.ds(at, rows)], sems.at[3 + n]))
        at += rows
    for copy in loads + copies:
        copy.start()
    for copy in loads:
        copy.wait()
    ones = jnp.ones((16, HD), BF16)
    row = lax.broadcasted_iota(jnp.int32, (16, BLOCK), 0)
    for b in range(SRC):
        prods = []
        for h in range(GROUP):
            cols = slice((b * GROUP + h) * HD, (b * GROUP + h + 1) * HD)
            qh, gh = q[:, cols], g[:, cols]
            pay[b, h * SUB : (h + 1) * SUB, :] = qh
            pay[b, BLOCK + h * SUB : BLOCK + (h + 1) * SUB, :] = gh
            prods.append(gh.astype(F32) * o[:, cols].astype(F32))
        prod = jnp.concatenate(prods, axis=0)
        high = prod.astype(BF16)
        low = (prod - high.astype(F32)).astype(BF16)
        d1, d2, d3 = pieces_of(dot(ones, high, NT) + dot(ones, low, NT))
        rows = jnp.where(row == 0, d1, jnp.where(row == 1, d2, jnp.where(row == 2, d3, 0.0)))
        pay[b, DROW:PAY, :] = rows.astype(BF16)
    for copy in copies:
        copy.wait()


def pack(*arrays):
    arrays = [pltpu.with_memory_space_constraint(a, pltpu.HBM) for a in arrays]
    return pl.pallas_call(
        pack_kernel,
        in_specs=[ANYSPEC] * 7,
        out_specs=[VSPEC, VSPEC],
        out_shape=[pltpu.VMEM((SRC, PAY, HD), BF16), pltpu.VMEM((2 * KW, HD), BF16)],
        scratch_shapes=[pltpu.VMEM((SUB, SRC * GROUP * HD), BF16)] * 3
        + [pltpu.SemaphoreType.DMA((7,))],
        compiler_params=pltpu.CompilerParams(vmem_limit_bytes=16 << 20),
        name="pack",
    )(*arrays)


def column(rows):
    line = jnp.concatenate([rows[s : s + 1, :] for s in range(SRC)], axis=1)
    return jnp.broadcast_to(line, (HD, QR)).T


def tiles_kernel(cfg, *refs):
    unit, far, first, last, more_g, more_dq, final = cfg
    refs = list(refs)

    def take(n):
        out = refs[:n]
        del refs[:n]
        return out

    place, lengths = take(2)
    pays = take(1 if unit == "own" else 2)
    key_in = take(last - first)
    take(1 if more_g else 0)
    dq_in = take(1 if more_dq else 0)
    sums = take(1)[0]
    split = final and unit in ("near_a", "near_b")
    dq_out = take(2 if split else 1)
    qs, gs, qt, gt, keys, log_col, delta_col, dqa = refs

    rows = QR // len(pays)
    scalars = []
    for n, pay in enumerate(pays):
        qs[n * rows : (n + 1) * rows, :] = pay[:, 0:BLOCK, :].reshape(rows, HD)
        gs[n * rows : (n + 1) * rows, :] = pay[:, BLOCK : 2 * BLOCK, :].reshape(rows, HD)
        scalars.append(pay[:, DROW:PAY, :].astype(F32))
    scalars = jnp.concatenate(scalars, axis=0)
    add = lambda n: scalars[:, n, :] + scalars[:, n + 1, :] + scalars[:, n + 2, :]
    delta_col[...] = column(add(0))
    log_col[...] = column(add(LROW - DROW))
    qt[...] = qs[...].T
    gt[...] = gs[...].T
    if more_dq:
        dqa[...] = dq_in[0][...]
    else:
        dqa[...] = jnp.zeros((QR, HD), F32)
    y, xh, c = place[0], place[1], place[2]

    def step(j, carry):
        for n in range(first, last):

            @pl.when(j == n)
            def _():
                keys[...] = key_in[n - first][...]

        def products(at, width, rows):
            s = dot(qs[:rows], keys[at : at + width, :], NT)
            dp = dot(gs[:rows], keys[KW + at : KW + at + width, :], NT)
            return s, dp

        def grads(at, width, rows, s, dp, allowed):
            wide = lambda col: jnp.concatenate([col[:rows]] * (width // HD), axis=1)
            p = jnp.exp2(s * C2 - wide(log_col))
            if allowed is not None:
                p = jnp.where(allowed, p, 0.0)
            ds = (p * (dp - wide(delta_col))).astype(BF16)
            p = p.astype(BF16)
            dk = dot(qt[:, :rows], ds, NN)
            dv = dot(gt[:, :rows], p, NN)
            cols = slice(at, at + width)
            if more_g or at >= PK:
                sums[j, 0:HD, cols] += dk
                sums[j, HD : 2 * HD, cols] += dv
            else:
                sums[j, 0:HD, cols] = dk
                sums[j, HD : 2 * HD, cols] = dv
            return dot(ds, keys[at : at + width, :], NN)

        if not more_g:
            sums[j, :, PK:KW] = jnp.zeros((2 * HD, RK), F32)
        part = 256
        total = None
        ahead = products(0, part, QR)
        for n in range(PK // part):
            s, dp = ahead
            if n + 1 < PK // part:
                ahead = products((n + 1) * part, part, QR)
            term = grads(n * part, part, QR, s, dp, None)
            total = term if total is None else total + term
        dqa[...] += total

        if unit != "opp":
            rows = QR if unit == "own" else QR // 2
            qi = 4 * (y if unit == "own" else (y + 1) % 4) + 2 * xh + c
            kj = 4 * y + 2 * ((1 - xh) if far else xh) + (c + j - 2 * c * j)
            seen, end = kj <= qi, 0
            for r in range(lengths.shape[0]):
                end = end + lengths[r]
                seen = seen & ((end <= kj) | (end > qi))

            @pl.when(seen)
            def _():
                allowed = None
                if unit == "own":
                    row = lax.broadcasted_iota(jnp.int32, (rows, RK), 0)
                    key_at = lax.broadcasted_iota(jnp.int32, (rows, RK), 1)
                    token = (row // BLOCK) * SUB + row % SUB
                    allowed = (kj < qi) | (key_at <= token)
                s, dp = products(PK, RK, rows)
                dqa[:rows, :] += grads(PK, RK, rows, s, dp, allowed)

        return carry

    lax.fori_loop(first, last, step, 0)
    if not more_g and last - first < 2:
        sums[1 - first] = jnp.zeros((2 * HD, KW), F32)
    if final and unit != "own":
        done = (dqa[...] * SCALE).astype(BF16).reshape(SRC, BLOCK, HD)
        if split:
            dq_out[0][...], dq_out[1][...] = done[0:4], done[4:8]
        else:
            dq_out[0][...] = done
    else:
        dq_out[0][...] = dqa[...]


def tiles(name, place, lengths, pays, keys, sums=None, dq=None, final=False):
    unit, where = name.rsplit("_", 1)
    first, last = {"mine": (0, 1), "core": (1, 2)}.get(where, (0, 2))
    cfg = (unit, where == "far", first, last, sums is not None, dq is not None, final)
    operands = held(*pays, *keys)
    aliases = {}
    if sums is not None:
        aliases[2 + len(operands)] = 0
        operands += held(sums)
    if dq is not None:
        if not final or unit == "own":
            aliases[2 + len(operands)] = 1
        operands += held(dq)
    if not final or unit == "own":
        dq_shapes = [pltpu.VMEM((QR, HD), F32)]
    elif unit == "opp":
        dq_shapes = [pltpu.VMEM((SRC, BLOCK, HD), BF16)]
    else:
        dq_shapes = [pltpu.VMEM((SRC // 2, BLOCK, HD), BF16)] * 2
    sums, *dqs = pl.pallas_call(
        functools.partial(tiles_kernel, cfg),
        in_specs=[SSPEC] * 2 + [VSPEC] * len(operands),
        out_specs=[VSPEC] * (1 + len(dq_shapes)),
        out_shape=[pltpu.VMEM((2, 2 * HD, KW), F32)] + dq_shapes,
        scratch_shapes=[
            pltpu.VMEM((QR, HD), BF16),
            pltpu.VMEM((QR, HD), BF16),
            pltpu.VMEM((HD, QR), BF16),
            pltpu.VMEM((HD, QR), BF16),
            pltpu.VMEM((2 * KW, HD), BF16),
            pltpu.VMEM((QR, HD), F32),
            pltpu.VMEM((QR, HD), F32),
            pltpu.VMEM((QR, HD), F32),
        ],
        input_output_aliases=aliases,
        compiler_params=pltpu.CompilerParams(vmem_limit_bytes=24 << 20),
        cost_estimate=pl.CostEstimate(
            flops=QR * PK * HD, bytes_accessed=1 << 18, transcendentals=0
        ),
        name=name,
    )(place, lengths, *operands)
    return sums, (dqs[0] if len(dqs) == 1 else dqs)


def finish_kernel(own, up_a, up_b, down_a, down_b, opp, out):
    for s in range(SRC):
        up, down = (up_a, down_a) if s < 4 else (up_b, down_b)
        rows = own[s * BLOCK : (s + 1) * BLOCK, :] * SCALE
        rows = rows + up[s % 4].astype(F32) + down[s % 4].astype(F32) + opp[s].astype(F32)
        out[s] = rows.astype(BF16)


def finish(*terms):
    return pl.pallas_call(
        finish_kernel,
        in_specs=[VSPEC] * 6,
        out_specs=VSPEC,
        out_shape=pltpu.VMEM((SRC, BLOCK, HD), BF16),
        name="finish",
    )(*held(*terms))


def close_kernel(own, core, chip, dk, dv, drk, drv):
    def total(rows, cols):
        part = own[0, rows, cols] + core[rows, cols] + chip[rows, cols].astype(F32)
        return part.T

    keys, values = slice(0, HD), slice(HD, 2 * HD)
    dk[...] = total(keys, slice(0, PK)) * SCALE
    drk[...] = total(keys, slice(PK, KW)) * SCALE
    dv[...] = total(values, slice(0, PK))
    drv[...] = total(values, slice(PK, KW))


def close(own, core, chip):
    shape = lambda rows: jax.ShapeDtypeStruct((rows, HD), F32)
    return pl.pallas_call(
        close_kernel,
        in_specs=[VSPEC] * 3,
        out_specs=[VSPEC] * 4,
        out_shape=[shape(PK), shape(PK), shape(RK), shape(RK)],
        compiler_params=pltpu.CompilerParams(vmem_limit_bytes=16 << 20),
        name="close",
    )(*held(own, core, chip))


def shift(n, s):
    return [(i, (i + s) % n) for i in range(n)]


def after(values, *earlier):
    return lax.optimization_barrier((values, earlier))[0]


def shards(
    queries,
    out_grad,
    attn_out,
    log_totals,
    prompt_keys,
    prompt_values,
    rollout_keys,
    rollout_values,
    rollout_blocks,
):
    place = jnp.stack([lax.axis_index(Y), lax.axis_index(XH), lax.axis_index(C)])
    place = place.astype(jnp.int32)
    to_next, to_last, swap = shift(4, 1), shift(4, -1), shift(2, 1)

    logs = (log_totals * LOG2E).reshape(SRC, SUB, GROUP).transpose(0, 2, 1).reshape(SRC, 1, BLOCK)
    l1 = lax.reduce_precision(logs, 8, 7)
    l2 = lax.reduce_precision(logs - l1, 8, 7)
    logs = [p.astype(BF16) for p in (l1, l2, logs - l1 - l2)]
    logs = jnp.concatenate(logs + [jnp.zeros((SRC, PAY - LROW - 3, BLOCK), BF16)], axis=1)

    payload, kv_own = pack(
        queries, out_grad, attn_out, prompt_keys, rollout_keys, prompt_values, rollout_values
    )
    kv_x = lax.ppermute(kv_own, XH, swap)
    kv_c = lax.ppermute(kv_own, C, swap)
    own = lax.all_to_all(payload, BULK, split_axis=0, concat_axis=0, tiled=True)
    kv_xc = lax.ppermute(kv_x, C, swap)
    own = own.at[:, LROW:PAY, :].set(logs)
    own_a, own_b = own[:4], own[4:]
    up_a = lax.ppermute(own_a, Y, to_last)
    down_b = lax.ppermute(own_b, Y, to_next)
    up_b = lax.ppermute(own_b, Y, to_last)
    down_a = lax.ppermute(own_a, Y, to_next)

    run = lambda name, *rest: tiles(name, place, rollout_blocks, *rest)
    far, here = [kv_x, kv_xc], [kv_own, kv_c]
    g_far, dq_own = run("own_far", [own], far)
    g_here, dq_own = run("own_core", [own], here[1:], None, dq_own)
    up_a, down_b = after((up_a, down_b), dq_own)
    opp_a = lax.ppermute(up_a, Y, to_last)
    opp_b = lax.ppermute(down_b, Y, to_next)
    g_far, dq_a = run("near_a_far", [up_a, down_b], far, g_far)
    up_b, down_a = after((up_b, down_a), dq_a)
    g_far, dq_b = run("near_b_far", [up_b, down_a], far, g_far)
    dq_a = after(dq_a, dq_b)
    g_here, (a_up, a_down) = run("near_a_here", [up_a, down_b], here, g_here, dq_a, True)
    from_a_down = lax.ppermute(a_up, Y, to_next)
    from_a_up = lax.ppermute(a_down, Y, to_last)
    opp_a, opp_b = after((opp_a, opp_b), a_up)
    g_far, dq_opp = run("opp_far", [opp_a, opp_b], far, g_far)
    from_core = lax.ppermute(g_far[1], C, swap)
    g_here, opp = run("opp_here", [opp_a, opp_b], here, g_here, dq_opp, True)
    from_opp = lax.ppermute(opp, Y, shift(4, 2))
    to_chip = (g_far[0] + after(from_core, opp)).astype(BF16)
    from_chip = lax.ppermute(to_chip, XH, swap)
    dq_b = after(dq_b, to_chip, from_a_down, from_a_up)
    g_here, (b_up, b_down) = run("near_b_here", [up_b, down_a], here, g_here, dq_b, True)
    from_b_down = lax.ppermute(b_up, Y, to_next)
    from_b_up = lax.ppermute(b_down, Y, to_last)
    from_c = lax.ppermute(g_here[1], C, swap)
    dq_own = after(dq_own, b_up)
    g_here, dq_own = run("own_mine", [own], here[:1], g_here, dq_own, True)
    dk, dv, drk, drv = close(g_here, from_c, from_chip)
    dq_own = after(dq_own, drk)

    dq = finish(dq_own, from_b_up, from_a_up, from_a_down, from_b_down, from_opp)
    dq = lax.all_to_all(dq, BULK, split_axis=0, concat_axis=0, tiled=True)
    query_grad = dq.reshape(SRC * GROUP, SUB, HD).transpose(1, 0, 2).reshape(SUB, SRC * GROUP * HD)
    return (query_grad, dk, dv, drk, drv)


def solution(mesh):
    fine = Mesh(mesh.devices.reshape(4, 2, 2, 4, 2), (Y, XH, C, Z, XL))
    hold, bulk = (Y, XH, C), (Z, XL)
    tokens = P(hold + bulk, None)
    split = P(hold, bulk)
    return jax.shard_map(
        shards,
        mesh=fine,
        in_specs=(tokens, tokens, tokens, split, split, split, split, split, P()),
        out_specs=(tokens, split, split, split, split),
        check_vma=False,
    )
```

```python
import functools

import jax
import jax.numpy as jnp
from jax import lax
from jax.experimental import pallas as pl
from jax.experimental.pallas import tpu as pltpu
from jax.sharding import Mesh
from jax.sharding import PartitionSpec as P

F32 = jnp.float32
BF16 = jnp.bfloat16
HD = 128
GROUP = 8
BLOCK = 128
NBLK = 16
PK = 1024
RK = 128
KW = PK + RK
QR = BLOCK * GROUP
SRC = 8
SUB = BLOCK // SRC
DROW = 2 * BLOCK
LROW = DROW + 8
PAY = LROW + 8
SCALE = HD ** (-0.5)
LOG2E = 1.4426950408889634
C2 = SCALE * LOG2E

NN = (((1,), (0,)), ((), ()))
NT = (((1,), (1,)), ((), ()))

Y, XH, C, Z, XL = "y", "xh", "c", "z", "xl"
BULK = (Z, XL)


def dot(a, b, dims):
    return lax.dot_general(a, b, dims, preferred_element_type=F32)


def held(*arrays):
    return [pltpu.with_memory_space_constraint(a, pltpu.VMEM) for a in arrays]


ANYSPEC = pl.BlockSpec(memory_space=pl.ANY)
VSPEC = pl.BlockSpec(memory_space=pltpu.VMEM)
SSPEC = pl.BlockSpec(memory_space=pltpu.SMEM)


def pieces_of(x):
    a = x.astype(BF16).astype(F32)
    b = (x - a).astype(BF16).astype(F32)
    return a, b, x - a - b


def pack_kernel(q_in, g_in, o_in, pay, q, g, o, sems):
    loads = [
        pltpu.make_async_copy(src, dst, sems.at[n])
        for n, (src, dst) in enumerate(((q_in, q), (g_in, g), (o_in, o)))
    ]
    for copy in loads:
        copy.start()
    for copy in loads:
        copy.wait()
    ones = jnp.ones((16, HD), BF16)
    row = lax.broadcasted_iota(jnp.int32, (16, BLOCK), 0)
    for b in range(SRC):
        prods = []
        for h in range(GROUP):
            cols = slice((b * GROUP + h) * HD, (b * GROUP + h + 1) * HD)
            qh, gh = q[:, cols], g[:, cols]
            pay[b, h * SUB : (h + 1) * SUB, :] = qh
            pay[b, BLOCK + h * SUB : BLOCK + (h + 1) * SUB, :] = gh
            prods.append(gh.astype(F32) * o[:, cols].astype(F32))
        prod = jnp.concatenate(prods, axis=0)
        high = prod.astype(BF16)
        low = (prod - high.astype(F32)).astype(BF16)
        d1, d2, d3 = pieces_of(dot(ones, high, NT) + dot(ones, low, NT))
        rows = jnp.where(row == 0, d1, jnp.where(row == 1, d2, jnp.where(row == 2, d3, 0.0)))
        pay[b, DROW:PAY, :] = rows.astype(BF16)


def in_hbm(arrays):
    return [pltpu.with_memory_space_constraint(a, pltpu.HBM) for a in arrays]


def pack(*arrays):
    return pl.pallas_call(
        pack_kernel,
        in_specs=[ANYSPEC] * 3,
        out_specs=VSPEC,
        out_shape=pltpu.VMEM((SRC, PAY, HD), BF16),
        scratch_shapes=[pltpu.VMEM((SUB, SRC * GROUP * HD), BF16)] * 3
        + [pltpu.SemaphoreType.DMA((3,))],
        compiler_params=pltpu.CompilerParams(vmem_limit_bytes=8 << 20),
        name="pack",
    )(*in_hbm(arrays))


def join_kernel(pk, rk, pv, rv, kv, sems):
    copies, at = [], 0
    for n, (src, rows) in enumerate(((pk, PK), (rk, RK), (pv, PK), (rv, RK))):
        copies.append(pltpu.make_async_copy(src, kv.at[pl.ds(at, rows)], sems.at[n]))
        at += rows
    for copy in copies:
        copy.start()
    for copy in copies:
        copy.wait()


def join(*arrays):
    return pl.pallas_call(
        join_kernel,
        in_specs=[ANYSPEC] * 4,
        out_specs=VSPEC,
        out_shape=pltpu.VMEM((2 * KW, HD), BF16),
        scratch_shapes=[pltpu.SemaphoreType.DMA((4,))],
        name="join",
    )(*in_hbm(arrays))


def column(rows):
    line = jnp.concatenate([rows[s : s + 1, :] for s in range(SRC)], axis=1)
    return jnp.broadcast_to(line, (HD, QR)).T


def pick(n, values):
    out = values[0]
    for m in range(1, len(values)):
        out = jnp.where(n == m, values[m], out)
    return out


def tiles_kernel(cfg, *refs):
    units, far, have, final = cfg
    nu = len(units)
    refs = list(refs)

    def take(n):
        out = refs[:n]
        del refs[:n]
        return out

    place, lengths = take(2)
    pays = [r for n in units for r in take(2 if n == 2 else 1)]
    key_in = take(2)
    take(have["dq"] + have["sums"] + have["out"])
    dqs, sums = take(2)
    out = take(1)[0] if final else None
    qs, gs, qt, gt, keys, scalars, log_col, delta_col = refs
    y, xh, c = place[0], place[1], place[2]

    def step(t, carry):
        u, j = t // 2, t % 2
        back = pick(u, units)
        at_pay = 0
        for n in range(nu):
            parts = pays[at_pay : at_pay + (2 if units[n] == 2 else 1)]
            at_pay += len(parts)

            @pl.when(t == 2 * n)
            def _():
                rows, srcs = QR // len(parts), SRC // len(parts)
                for m, pay in enumerate(parts):
                    span = slice(m * rows, (m + 1) * rows)
                    qs[span, :] = pay[:, 0:BLOCK, :].reshape(rows, HD)
                    gs[span, :] = pay[:, BLOCK : 2 * BLOCK, :].reshape(rows, HD)
                    scalars[m * srcs : (m + 1) * srcs] = pay[:, DROW:PAY, :].astype(F32)

        @pl.when(j == 0)
        def _():
            add = lambda n: scalars[:, n, :] + scalars[:, n + 1, :] + scalars[:, n + 2, :]
            delta_col[...] = column(add(0))
            log_col[...] = column(add(LROW - DROW))
            qt[...] = qs[...].T
            gt[...] = gs[...].T
            if not have["started"]:
                dqs[back] = jnp.zeros((QR, HD), F32)

        for n in range(2):

            @pl.when(j == n)
            def _():
                keys[...] = key_in[n][...]

        def products(at, width):
            s = dot(qs[...], keys[at : at + width, :], NT)
            dp = dot(gs[...], keys[KW + at : KW + at + width, :], NT)
            return s, dp

        def grads(at, width, s, dp, allowed):
            wide = lambda col: jnp.concatenate([col[...]] * (width // HD), axis=1)
            p = jnp.exp2(s * C2 - wide(log_col))
            if allowed is not None:
                p = jnp.where(allowed, p, 0.0)
            ds = (p * (dp - wide(delta_col))).astype(BF16)
            p = p.astype(BF16)
            dk = dot(qt[...], ds, NN)
            dv = dot(gt[...], p, NN)
            cols = slice(at, at + width)
            if have["sums"] or at >= PK:
                sums[j, 0:HD, cols] += dk
                sums[j, HD : 2 * HD, cols] += dv
            else:
                sums[j, 0:HD, cols] = dk
                sums[j, HD : 2 * HD, cols] = dv
            return dot(ds, keys[at : at + width, :], NN)

        if not have["sums"]:
            sums[j, :, PK:KW] = jnp.zeros((2 * HD, RK), F32)
        part = 256
        total = None
        ahead = products(0, part)
        for n in range(PK // part):
            s, dp = ahead
            if n + 1 < PK // part:
                ahead = products((n + 1) * part, part)
            term = grads(n * part, part, s, dp, None)
            total = term if total is None else total + term
        dqs[back] += total

        qi = 4 * ((y + back) % 4) + 2 * xh + c
        kj = 4 * y + 2 * ((1 - xh) if far else xh) + (c + j - 2 * c * j)
        seen, end = kj <= qi, 0
        for r in range(lengths.shape[0]):
            end = end + lengths[r]
            seen = seen & ((end <= kj) | (end > qi))

        @pl.when(seen)
        def _():
            row = lax.broadcasted_iota(jnp.int32, (QR, RK), 0)
            key_at = lax.broadcasted_iota(jnp.int32, (QR, RK), 1)
            token = (row // BLOCK) * SUB + row % SUB
            allowed = (kj < qi) | (key_at <= token)
            s, dp = products(PK, RK)
            dqs[back] += grads(PK, RK, s, dp, allowed)

        if final:

            @pl.when(j == 1)
            def _():
                done = (dqs[back] * SCALE).astype(BF16)
                out[(y + back) % 4] = done.reshape(SRC, BLOCK, HD)

        return carry

    lax.fori_loop(0, 2 * nu, step, 0)


def tiles(name, units, far, place, lengths, pays, keys, dqs, sums, out=None, started=False, final=False):
    have = {"dq": dqs is not None, "sums": sums is not None, "out": out is not None, "started": started}
    operands = held(*pays, *keys)
    aliases = {}
    for n, state in enumerate((dqs, sums, out)):
        if state is not None:
            aliases[2 + len(operands)] = n
            operands += held(state)
    shapes = [pltpu.VMEM((4, QR, HD), F32), pltpu.VMEM((2, 2 * HD, KW), F32)]
    if final:
        shapes.append(pltpu.VMEM((4, SRC, BLOCK, HD), BF16))
    return pl.pallas_call(
        functools.partial(tiles_kernel, (tuple(units), far, have, final)),
        in_specs=[SSPEC] * 2 + [VSPEC] * len(operands),
        out_specs=[VSPEC] * len(shapes),
        out_shape=shapes,
        scratch_shapes=[
            pltpu.VMEM((QR, HD), BF16),
            pltpu.VMEM((QR, HD), BF16),
            pltpu.VMEM((HD, QR), BF16),
            pltpu.VMEM((HD, QR), BF16),
            pltpu.VMEM((2 * KW, HD), BF16),
            pltpu.VMEM((SRC, PAY - DROW, HD), F32),
            pltpu.VMEM((QR, HD), F32),
            pltpu.VMEM((QR, HD), F32),
        ],
        input_output_aliases=aliases,
        compiler_params=pltpu.CompilerParams(vmem_limit_bytes=24 << 20),
        cost_estimate=pl.CostEstimate(
            flops=1, bytes_accessed=1, transcendentals=0
        ),
        name=name,
    )(place, lengths, *operands)


def finish_kernel(parts, out):
    for b in range(SRC):
        for h in range(GROUP):
            rows = slice(h * SUB, (h + 1) * SUB)
            terms = [parts[n * SRC + b, rows, :].astype(F32) for n in range(4)]
            col = (b * GROUP + h) * HD
            out[:, col : col + HD] = (terms[0] + terms[1] + terms[2] + terms[3]).astype(BF16)


def finish(parts):
    return pl.pallas_call(
        finish_kernel,
        in_specs=[VSPEC],
        out_specs=VSPEC,
        out_shape=jax.ShapeDtypeStruct((SUB, SRC * GROUP * HD), BF16),
        name="finish",
    )(*held(parts))


def close_kernel(own, core, chip, dk, dv, drk, drv):
    def total(rows, cols):
        part = own[0, rows, cols] + core[rows, cols] + chip[rows, cols].astype(F32)
        return part.T

    keys, values = slice(0, HD), slice(HD, 2 * HD)
    dk[...] = total(keys, slice(0, PK)) * SCALE
    drk[...] = total(keys, slice(PK, KW)) * SCALE
    dv[...] = total(values, slice(0, PK))
    drv[...] = total(values, slice(PK, KW))


def close(own, core, chip):
    shape = lambda rows: jax.ShapeDtypeStruct((rows, HD), F32)
    return pl.pallas_call(
        close_kernel,
        in_specs=[VSPEC] * 3,
        out_specs=[VSPEC] * 4,
        out_shape=[shape(PK), shape(PK), shape(RK), shape(RK)],
        compiler_params=pltpu.CompilerParams(vmem_limit_bytes=16 << 20),
        name="close",
    )(*held(own, core, chip))


def shift(n, s):
    return [(i, (i + s) % n) for i in range(n)]


def after(values, *earlier):
    return lax.optimization_barrier((values, earlier))[0]


def shards(
    queries,
    out_grad,
    attn_out,
    log_totals,
    prompt_keys,
    prompt_values,
    rollout_keys,
    rollout_values,
    rollout_blocks,
):
    place = jnp.stack([lax.axis_index(Y), lax.axis_index(XH), lax.axis_index(C)])
    place = place.astype(jnp.int32)
    to_next, to_last, swap = shift(4, 1), shift(4, -1), shift(2, 1)

    logs = (log_totals * LOG2E).reshape(SRC, SUB, GROUP).transpose(0, 2, 1).reshape(SRC, 1, BLOCK)
    l1 = lax.reduce_precision(logs, 8, 7)
    l2 = lax.reduce_precision(logs - l1, 8, 7)
    logs = [p.astype(BF16) for p in (l1, l2, logs - l1 - l2)]
    logs = jnp.concatenate(logs + [jnp.zeros((SRC, PAY - LROW - 3, BLOCK), BF16)], axis=1)

    payload = pack(queries, out_grad, attn_out)
    own = lax.all_to_all(payload, BULK, split_axis=0, concat_axis=0, tiled=True)
    kv_own = join(*after((prompt_keys, rollout_keys, prompt_values, rollout_values), payload))
    kv_x = lax.ppermute(kv_own, XH, swap)
    kv_c = lax.ppermute(kv_own, C, swap)
    kv_xc = lax.ppermute(kv_x, C, swap)
    own = own.at[:, LROW:PAY, :].set(logs)
    up = lax.ppermute(own, Y, to_last)
    down = lax.ppermute(own, Y, to_next)

    def run(name, units, far, *rest, **kw):
        keys = [kv_x, kv_xc] if far else [kv_own, kv_c]
        return tiles(name, units, far, place, rollout_blocks, rest[0], keys, *rest[1:], **kw)

    dqs, g_here = run("own_here", [0], False, [own], None, None)
    dqs, g_far, out = run("own_far", [0], True, [own], dqs, None, started=True, final=True)
    up, down = after((up, down), out)
    opp = [lax.ppermute(up[: SRC // 2], Y, to_last), lax.ppermute(down[SRC // 2 :], Y, to_next)]
    dqs, g_far = run("near_far", [1, 3], True, [up, down], dqs, g_far)
    opp = after(opp, dqs)
    dqs, g_far = run("opp_far", [2], True, opp, dqs, g_far)
    from_core = lax.ppermute(g_far[1], C, swap)
    dqs, g_here, out = run("up_here", [1], False, [up], dqs, g_here, out, started=True, final=True)
    to_chip = (g_far[0] + after(from_core, dqs)).astype(BF16)
    from_chip = lax.ppermute(to_chip, XH, swap)
    dqs = after(dqs, to_chip)
    dqs, g_here, out = run(
        "rest_here", [3, 2], False, [down, *opp], dqs, g_here, out, started=True, final=True
    )
    from_c = lax.ppermute(g_here[1], C, swap)
    parts = lax.all_to_all(
        out.reshape(4 * SRC, BLOCK, HD), (Y,) + BULK, split_axis=0, concat_axis=0, tiled=True
    )
    dk, dv, drk, drv = close(g_here, from_c, from_chip)
    query_grad = finish(after(parts, dk))
    return (query_grad, dk, dv, drk, drv)


def solution(mesh):
    fine = Mesh(mesh.devices.reshape(4, 2, 2, 4, 2), (Y, XH, C, Z, XL))
    hold, bulk = (Y, XH, C), (Z, XL)
    tokens = P(hold + bulk, None)
    split = P(hold, bulk)
    return jax.shard_map(
        shards,
        mesh=fine,
        in_specs=(tokens, tokens, tokens, split, split, split, split, split, P()),
        out_specs=(tokens, split, split, split, split),
        check_vma=False,
    )
```

```python
import functools

import jax
import jax.numpy as jnp
from jax import lax
from jax.experimental import pallas as pl
from jax.experimental.pallas import tpu as pltpu
from jax.sharding import Mesh
from jax.sharding import PartitionSpec as P

F32 = jnp.float32
BF16 = jnp.bfloat16
HD = 128
GROUP = 8
BLOCK = 128
NBLK = 16
PK = 1024
RK = 128
KW = PK + RK
QR = BLOCK * GROUP
SRC = 8
SUB = BLOCK // SRC
DROW = 2 * BLOCK
LROW = DROW + 8
PAY = LROW + 8
SCALE = HD ** (-0.5)
LOG2E = 1.4426950408889634
C2 = SCALE * LOG2E

NN = (((1,), (0,)), ((), ()))
NT = (((1,), (1,)), ((), ()))

Y, XH, C, Z, XL = "y", "xh", "c", "z", "xl"
BULK = (Z, XL)


def dot(a, b, dims):
    return lax.dot_general(a, b, dims, preferred_element_type=F32)


def held(*arrays):
    return [pltpu.with_memory_space_constraint(a, pltpu.VMEM) for a in arrays]


ANYSPEC = pl.BlockSpec(memory_space=pl.ANY)
VSPEC = pl.BlockSpec(memory_space=pltpu.VMEM)
SSPEC = pl.BlockSpec(memory_space=pltpu.SMEM)


def pieces_of(x):
    a = x.astype(BF16).astype(F32)
    b = (x - a).astype(BF16).astype(F32)
    return a, b, x - a - b


def pack_kernel(place, q_in, g_in, o_in, pay, q, g, o, sems):
    loads = [
        pltpu.make_async_copy(src, dst, sems.at[n])
        for n, (src, dst) in enumerate(((q_in, q), (g_in, g), (o_in, o)))
    ]
    for copy in loads:
        copy.start()
    for copy in loads:
        copy.wait()
    ones = jnp.ones((16, HD), BF16)
    row = lax.broadcasted_iota(jnp.int32, (16, BLOCK), 0)
    for b in range(SRC):
        prods = []
        for h in range(GROUP):
            cols = slice((b * GROUP + h) * HD, (b * GROUP + h + 1) * HD)
            qh, gh = q[:, cols], g[:, cols]
            pay[b, h * SUB : (h + 1) * SUB, :] = qh
            pay[b, BLOCK + h * SUB : BLOCK + (h + 1) * SUB, :] = gh
            prods.append(gh.astype(F32) * o[:, cols].astype(F32))
        prod = jnp.concatenate(prods, axis=0)
        high = prod.astype(BF16)
        low = (prod - high.astype(F32)).astype(BF16)
        d1, d2, d3 = pieces_of(dot(ones, high, NT) + dot(ones, low, NT))
        rows = jnp.where(row == 0, d1, jnp.where(row == 1, d2, jnp.where(row == 2, d3, 0.0)))
        pay[b, DROW:PAY, :] = rows.astype(BF16)


def in_hbm(arrays):
    return [pltpu.with_memory_space_constraint(a, pltpu.HBM) for a in arrays]


def pack(place, *arrays):
    return pl.pallas_call(
        pack_kernel,
        in_specs=[SSPEC] + [ANYSPEC] * 3,
        out_specs=VSPEC,
        out_shape=pltpu.VMEM((SRC, PAY, HD), BF16),
        scratch_shapes=[pltpu.VMEM((SUB, SRC * GROUP * HD), BF16)] * 3
        + [pltpu.SemaphoreType.DMA((3,))],
        compiler_params=pltpu.CompilerParams(vmem_limit_bytes=8 << 20),
        name="pack",
    )(place, *in_hbm(arrays))


def join_kernel(pk, rk, pv, rv, kv, sems):
    copies, at = [], 0
    for n, (src, rows) in enumerate(((pk, PK), (rk, RK), (pv, PK), (rv, RK))):
        copies.append(pltpu.make_async_copy(src, kv.at[pl.ds(at, rows)], sems.at[n]))
        at += rows
    for copy in copies:
        copy.start()
    for copy in copies:
        copy.wait()


def join(*arrays):
    return pl.pallas_call(
        join_kernel,
        in_specs=[ANYSPEC] * 4,
        out_specs=VSPEC,
        out_shape=pltpu.VMEM((2 * KW, HD), BF16),
        scratch_shapes=[pltpu.SemaphoreType.DMA((4,))],
        compiler_params=pltpu.CompilerParams(vmem_limit_bytes=4 << 20),
        name="join",
    )(*in_hbm(arrays))


def column(rows):
    line = jnp.concatenate([rows[s : s + 1, :] for s in range(SRC)], axis=1)
    return jnp.broadcast_to(line, (HD, QR)).T


def tiles_kernel(cfg, *refs):
    unit, keys_of, have_sums, have_dq, final, others = cfg
    nk = len(keys_of)
    refs = list(refs)

    def take(n):
        out = refs[:n]
        del refs[:n]
        return out

    place, lengths, pay = take(3)
    keys = take(nk)
    sums_in = [take(1)[0] if h else None for h in have_sums]
    dq_in = take(1)[0] if have_dq else None
    blocks = take(others)
    sums = take(nk)
    dq_out, qs, gs, qt, gt, log_col, delta_col, dqa, done, sems = refs
    dq = dqa if final else dq_out
    copies = [
        pltpu.make_async_copy(block, dq_out.at[(place[0] + n) % 4], sems.at[n])
        for n, block in zip((0, 1, 3), blocks)
    ]
    for copy in copies:
        copy.start()

    qs[...] = pay[:, 0:BLOCK, :].reshape(QR, HD)
    gs[...] = pay[:, BLOCK : 2 * BLOCK, :].reshape(QR, HD)
    scalars = pay[:, DROW:PAY, :].astype(F32)
    add3 = lambda n: scalars[:, n, :] + scalars[:, n + 1, :] + scalars[:, n + 2, :]
    delta_col[...] = column(add3(0))
    log_col[...] = column(add3(LROW - DROW))
    qt[...] = qs[...].T
    gt[...] = gs[...].T
    for j in range(nk):
        tail = sums_in[j][:, PK:KW] if have_sums[j] else jnp.zeros((2 * HD, RK), F32)
        sums[j][:, PK:KW] = tail

    def products(j, at, width):
        s = dot(qs[...], keys[j][at : at + width, :], NT)
        dp = dot(gs[...], keys[j][KW + at : KW + at + width, :], NT)
        return s, dp

    def grads(j, at, width, s, dp, allowed, old):
        wide = lambda col: jnp.concatenate([col[...]] * (width // HD), axis=1)
        p = jnp.exp2(s * C2 - wide(log_col))
        if allowed is not None:
            p = jnp.where(allowed, p, 0.0)
        ds = (p * (dp - wide(delta_col))).astype(BF16)
        p = p.astype(BF16)
        cols = slice(at, at + width)
        for rows, left, right in ((slice(0, HD), qt, ds), (slice(HD, 2 * HD), gt, p)):
            term = dot(left[...], right, NN)
            sums[j][rows, cols] = term if old is None else old[rows, cols] + term
        return dot(ds, keys[j][at : at + width, :], NN)

    part, total = 256, None
    chunks = [(j, at) for j in range(nk) for at in range(0, PK, part)]
    ahead = products(*chunks[0], part)
    for m, (j, at) in enumerate(chunks):
        s, dp = ahead
        if m + 1 < len(chunks):
            ahead = products(*chunks[m + 1], part)
        term = grads(j, at, part, s, dp, None, sums_in[j])
        total = term if total is None else total + term
        if at + part == PK:
            old = dq if j else dq_in
            dq[...] = total if old is None else old[...] + total
            total = None

    if unit in ("own", "up"):
        y, xh, c = place[0], place[1], place[2]
        qi = 4 * (y if unit == "own" else (y + 1) % 4) + 2 * xh + c
        for j, (other_chip, other_core) in enumerate(keys_of):
            kj = 4 * y + 2 * ((1 - xh) if other_chip else xh) + ((1 - c) if other_core else c)
            seen, end = kj <= qi, 0
            for r in range(lengths.shape[0]):
                end = end + lengths[r]
                seen = seen & ((end <= kj) | (end > qi))

            @pl.when(seen)
            def _():
                allowed = None
                if unit == "own":
                    row = lax.broadcasted_iota(jnp.int32, (QR, RK), 0)
                    key_at = lax.broadcasted_iota(jnp.int32, (QR, RK), 1)
                    token = (row // BLOCK) * SUB + row % SUB
                    allowed = (kj < qi) | (key_at <= token)
                s, dp = products(j, PK, RK)
                dq[...] += grads(j, PK, RK, s, dp, allowed, sums[j])

    if final:
        rounded = (dq[...] * SCALE).astype(BF16).reshape(SRC, BLOCK, HD)
        if others:
            done[...] = rounded
            last = pltpu.make_async_copy(done, dq_out.at[(place[0] + 2) % 4], sems.at[2])
            last.start()
            for copy in copies + [last]:
                copy.wait()
        else:
            dq_out[...] = rounded


def tiles(name, unit, place, lengths, pay, keys_of, keys, sums, dq=None, final=False, others=()):
    have_sums = tuple(g is not None for g in sums)
    operands = held(pay, *keys)
    aliases = {}
    for n, old in enumerate(list(sums) + [dq]):
        if old is not None:
            if n < len(keys) or not final:
                aliases[2 + len(operands)] = n
            operands += held(old)
    operands += held(*others)
    dq_shape = pltpu.VMEM((SRC, BLOCK, HD), BF16) if final else pltpu.VMEM((QR, HD), F32)
    if others:
        dq_shape = pltpu.HBM((4, SRC, BLOCK, HD), BF16)
    shapes = [pltpu.VMEM((2 * HD, KW), F32)] * len(keys) + [dq_shape]
    *sums, dq = pl.pallas_call(
        functools.partial(tiles_kernel, (unit, tuple(keys_of), have_sums, dq is not None, final, len(others))),
        in_specs=[SSPEC] * 2 + [VSPEC] * len(operands),
        out_specs=[VSPEC] * len(keys) + [ANYSPEC if others else VSPEC],
        out_shape=shapes,
        scratch_shapes=[
            pltpu.VMEM((QR, HD), BF16),
            pltpu.VMEM((QR, HD), BF16),
            pltpu.VMEM((HD, QR), BF16),
            pltpu.VMEM((HD, QR), BF16),
            pltpu.VMEM((QR, HD), F32),
            pltpu.VMEM((QR, HD), F32),
            pltpu.VMEM((QR, HD) if final else (8, HD), F32),
            pltpu.VMEM((SRC, BLOCK, HD) if others else (1, 16, HD), BF16),
            pltpu.SemaphoreType.DMA((4,)),
        ],
        input_output_aliases=aliases,
        compiler_params=pltpu.CompilerParams(vmem_limit_bytes=14 << 20),
        cost_estimate=pl.CostEstimate(flops=1, bytes_accessed=1, transcendentals=0),
        name=name,
    )(place, lengths, *operands)
    return sums, dq


def finish_kernel(parts, out):
    for b in range(SRC):
        for h in range(GROUP):
            rows = slice(h * SUB, (h + 1) * SUB)
            terms = [parts[n * SRC + b, rows, :].astype(F32) for n in range(4)]
            col = (b * GROUP + h) * HD
            out[:, col : col + HD] = (terms[0] + terms[1] + terms[2] + terms[3]).astype(BF16)


def finish(parts):
    return pl.pallas_call(
        finish_kernel,
        in_specs=[VSPEC],
        out_specs=VSPEC,
        out_shape=jax.ShapeDtypeStruct((SUB, SRC * GROUP * HD), BF16),
        name="finish",
    )(*held(parts))


def close_kernel(own, core, chip_in, dk, dv, drk, drv, chip, sem):
    load = pltpu.make_async_copy(chip_in, chip, sem)
    load.start()
    load.wait()

    def total(rows, cols):
        part = own[rows, cols] + core[rows, cols] + chip[rows, cols].astype(F32)
        return part.T

    keys, values = slice(0, HD), slice(HD, 2 * HD)
    dk[...] = total(keys, slice(0, PK)) * SCALE
    drk[...] = total(keys, slice(PK, KW)) * SCALE
    dv[...] = total(values, slice(0, PK))
    drv[...] = total(values, slice(PK, KW))


def close(own, core, chip):
    shape = lambda rows: jax.ShapeDtypeStruct((rows, HD), F32)
    return pl.pallas_call(
        close_kernel,
        in_specs=[VSPEC, VSPEC, ANYSPEC],
        out_specs=[VSPEC] * 4,
        out_shape=[shape(PK), shape(PK), shape(RK), shape(RK)],
        scratch_shapes=[pltpu.VMEM((2 * HD, KW), BF16), pltpu.SemaphoreType.DMA],
        compiler_params=pltpu.CompilerParams(vmem_limit_bytes=16 << 20),
        name="close",
    )(*held(own, core), *in_hbm([chip]))


def shift(n, s):
    return [(i, (i + s) % n) for i in range(n)]


def after(values, *earlier):
    return lax.optimization_barrier((values, earlier))[0]


def shards(
    queries,
    out_grad,
    attn_out,
    log_totals,
    prompt_keys,
    prompt_values,
    rollout_keys,
    rollout_values,
    rollout_blocks,
):
    place = jnp.stack([lax.axis_index(Y), lax.axis_index(XH), lax.axis_index(C)])
    place = place.astype(jnp.int32)
    to_next, to_last, swap = shift(4, 1), shift(4, -1), shift(2, 1)

    logs = (log_totals * LOG2E).reshape(SRC, SUB, GROUP).transpose(0, 2, 1).reshape(SRC, 1, BLOCK)
    l1 = lax.reduce_precision(logs, 8, 7)
    l2 = lax.reduce_precision(logs - l1, 8, 7)
    logs = [p.astype(BF16) for p in (l1, l2, logs - l1 - l2)]
    logs = jnp.concatenate(logs + [jnp.zeros((SRC, PAY - LROW - 3, BLOCK), BF16)], axis=1)

    payload = pack(place, queries, out_grad, attn_out)
    own = lax.all_to_all(payload, BULK, split_axis=0, concat_axis=0, tiled=True)
    kv_own = join(*after((prompt_keys, rollout_keys, prompt_values, rollout_values), payload))
    kv_c = lax.ppermute(kv_own, C, swap)
    kv_x = lax.ppermute(after(kv_own, own), XH, swap)
    own = own.at[:, LROW:PAY, :].set(logs)
    up = lax.ppermute(own, Y, to_last)
    down = lax.ppermute(own, Y, to_next)

    def run(name, pay, keys_of, keys, sums, dq=None, final=False, others=()):
        unit = name.split("_")[0]
        return tiles(name, unit, place, rollout_blocks, pay, keys_of, keys, sums, dq, final, others)

    o_own, o_core, o_chip, o_both = (0, 0), (0, 1), (1, 0), (1, 1)
    here, far = [o_own, o_core], [o_chip, o_both]
    (g_own, g_c), dq_own = run("own_here", own, here, [kv_own, kv_c], [None, None])
    kv_x = after(kv_x, dq_own)
    kv_xc = lax.ppermute(kv_x, C, swap)
    (g_x,), dq_own = run("own_chip", own, [o_chip], [kv_x], [None], dq_own)
    up, down = after((up, down), dq_own)
    opp = lax.ppermute(after(own, up, down), Y, shift(4, 2))
    (g_xc,), dq_own = run("own_both", own, [o_both], [kv_xc], [None], dq_own, True)
    up = after(up, dq_own)
    (g_x, g_xc), dq_up = run("up_far", up, far, [kv_x, kv_xc], [g_x, g_xc])
    (g_x, g_xc), dq_down = run("down_far", down, far, [kv_x, kv_xc], [g_x, g_xc])
    (g_xc,), dq_opp = run("opp_both", opp, [o_both], [kv_xc], [g_xc])
    from_core = lax.ppermute(g_xc, C, swap)
    (g_x,), dq_opp = run("opp_chip", opp, [o_chip], [kv_x], [g_x], dq_opp)
    to_chip = (g_x + after(from_core, dq_opp)).astype(BF16)
    from_chip = lax.ppermute(to_chip, XH, swap)
    dq_up = after(dq_up, to_chip)
    (g_own, g_c), dq_up = run("up_here", up, here, [kv_own, kv_c], [g_own, g_c], dq_up, True)
    (g_own, g_c), dq_down = run(
        "down_here", down, here, [kv_own, kv_c], [g_own, g_c], dq_down, True
    )
    (g_own, g_c), dq = run(
        "opp_here", opp, here, [kv_own, kv_c], [g_own, g_c], dq_opp, True, [dq_own, dq_up, dq_down]
    )
    from_c = lax.ppermute(g_c, C, swap)
    dq, from_chip = lax.optimization_barrier((dq, from_chip))
    dq = dq.reshape(4 * SRC, BLOCK, HD)
    parts = lax.all_to_all(dq, (Y,) + BULK, split_axis=0, concat_axis=0, tiled=True)
    dk, dv, drk, drv = close(g_own, from_c, from_chip)
    query_grad = finish(after(parts, dk))
    return (query_grad, dk, dv, drk, drv)


def solution(mesh):
    fine = Mesh(mesh.devices.reshape(4, 2, 2, 4, 2), (Y, XH, C, Z, XL))
    hold, bulk = (Y, XH, C), (Z, XL)
    tokens = P(hold + bulk, None)
    split = P(hold, bulk)
    return jax.shard_map(
        shards,
        mesh=fine,
        in_specs=(tokens, tokens, tokens, split, split, split, split, split, P()),
        out_specs=(tokens, split, split, split, split),
        check_vma=False,
    )
```

```python
import functools

import jax
import jax.numpy as jnp
from jax import lax
from jax.experimental import pallas as pl
from jax.experimental.pallas import tpu as pltpu
from jax.sharding import Mesh
from jax.sharding import PartitionSpec as P

F32 = jnp.float32
BF16 = jnp.bfloat16
HD = 128
GROUP = 8
BLOCK = 128
NBLK = 16
PK = 1024
RK = 128
KW = PK + RK
QR = BLOCK * GROUP
SRC = 8
SUB = BLOCK // SRC
DROW = 2 * BLOCK
LROW = DROW + 8
PAY = LROW + 8
SCALE = HD ** (-0.5)
LOG2E = 1.4426950408889634
C2 = SCALE * LOG2E

NN = (((1,), (0,)), ((), ()))
NT = (((1,), (1,)), ((), ()))

Y, XH, C, Z, XL = "y", "xh", "c", "z", "xl"
BULK = (Z, XL)


def dot(a, b, dims):
    return lax.dot_general(a, b, dims, preferred_element_type=F32)


def held(*arrays):
    return [pltpu.with_memory_space_constraint(a, pltpu.VMEM) for a in arrays]


ANYSPEC = pl.BlockSpec(memory_space=pl.ANY)
VSPEC = pl.BlockSpec(memory_space=pltpu.VMEM)
SSPEC = pl.BlockSpec(memory_space=pltpu.SMEM)


def pieces_of(x):
    a = x.astype(BF16).astype(F32)
    b = (x - a).astype(BF16).astype(F32)
    return a, b, x - a - b


def pack_kernel(place, q_in, g_in, o_in, pay, q, g, o, sems):
    loads = [
        pltpu.make_async_copy(src, dst, sems.at[n])
        for n, (src, dst) in enumerate(((q_in, q), (g_in, g), (o_in, o)))
    ]
    for copy in loads:
        copy.start()
    for copy in loads:
        copy.wait()
    ones = jnp.ones((16, HD), BF16)
    row = lax.broadcasted_iota(jnp.int32, (16, BLOCK), 0)
    for b in range(SRC):
        prods = []
        for h in range(GROUP):
            cols = slice((b * GROUP + h) * HD, (b * GROUP + h + 1) * HD)
            qh, gh = q[:, cols], g[:, cols]
            pay[b, h * SUB : (h + 1) * SUB, :] = qh
            pay[b, BLOCK + h * SUB : BLOCK + (h + 1) * SUB, :] = gh
            prods.append(gh.astype(F32) * o[:, cols].astype(F32))
        prod = jnp.concatenate(prods, axis=0)
        high = prod.astype(BF16)
        low = (prod - high.astype(F32)).astype(BF16)
        d1, d2, d3 = pieces_of(dot(ones, high, NT) + dot(ones, low, NT))
        rows = jnp.where(row == 0, d1, jnp.where(row == 1, d2, jnp.where(row == 2, d3, 0.0)))
        pay[b, DROW:PAY, :] = rows.astype(BF16)


def in_hbm(arrays):
    return [pltpu.with_memory_space_constraint(a, pltpu.HBM) for a in arrays]


def pack(place, *arrays):
    return pl.pallas_call(
        pack_kernel,
        in_specs=[SSPEC] + [ANYSPEC] * 3,
        out_specs=VSPEC,
        out_shape=pltpu.VMEM((SRC, PAY, HD), BF16),
        scratch_shapes=[pltpu.VMEM((SUB, SRC * GROUP * HD), BF16)] * 3
        + [pltpu.SemaphoreType.DMA((3,))],
        compiler_params=pltpu.CompilerParams(vmem_limit_bytes=8 << 20),
        name="pack",
    )(place, *in_hbm(arrays))


def join_kernel(pk, rk, pv, rv, kv, sems):
    copies, at = [], 0
    for n, (src, rows) in enumerate(((pk, PK), (rk, RK), (pv, PK), (rv, RK))):
        copies.append(pltpu.make_async_copy(src, kv.at[pl.ds(at, rows)], sems.at[n]))
        at += rows
    for copy in copies:
        copy.start()
    for copy in copies:
        copy.wait()


def join(*arrays):
    return pl.pallas_call(
        join_kernel,
        in_specs=[ANYSPEC] * 4,
        out_specs=VSPEC,
        out_shape=pltpu.VMEM((2 * KW, HD), BF16),
        scratch_shapes=[pltpu.SemaphoreType.DMA((4,))],
        compiler_params=pltpu.CompilerParams(vmem_limit_bytes=4 << 20),
        name="join",
    )(*in_hbm(arrays))


def column(rows):
    line = jnp.concatenate([rows[s : s + 1, :] for s in range(SRC)], axis=1)
    return jnp.broadcast_to(line, (HD, QR)).T


def tiles_kernel(cfg, *refs):
    unit, keys_of, have_sums, have_dq, final, others = cfg
    nk = len(keys_of)
    refs = list(refs)

    def take(n):
        out = refs[:n]
        del refs[:n]
        return out

    place, lengths = take(2)
    pays = take(2 if unit == "near" else 1)
    rows_all = QR * len(pays)
    keys = take(nk)
    sums_in = [take(1)[0] if h else None for h in have_sums]
    dq_in = take(1)[0] if have_dq else None
    blocks = take(others)
    sums = take(nk)
    dq_out, qs, gs, qt, gt, log_col, delta_col, dqa, done, sems = refs
    dq = dqa if final else dq_out
    copies = []
    if blocks:
        parts = ((0, blocks[0]), (1, blocks[1].at[0]), (3, blocks[1].at[1]))
        for n, (back, block) in enumerate(parts):
            target = dq_out.at[(place[0] + back) % 4]
            copies.append(pltpu.make_async_copy(block, target, sems.at[n]))
    for copy in copies:
        copy.start()

    for m, pay in enumerate(pays):
        rows = slice(m * QR, (m + 1) * QR)
        qs[rows, :] = pay[:, 0:BLOCK, :].reshape(QR, HD)
        gs[rows, :] = pay[:, BLOCK : 2 * BLOCK, :].reshape(QR, HD)
        scalars = pay[:, DROW:PAY, :].astype(F32)
        add3 = lambda n: scalars[:, n, :] + scalars[:, n + 1, :] + scalars[:, n + 2, :]
        delta_col[rows, :] = column(add3(0))
        log_col[rows, :] = column(add3(LROW - DROW))
    qt[...] = qs[...].T
    gt[...] = gs[...].T
    for j in range(nk):
        tail = sums_in[j][:, PK:KW] if have_sums[j] else jnp.zeros((2 * HD, RK), F32)
        sums[j][:, PK:KW] = tail

    def products(j, at, width, rows):
        s = dot(qs[:rows], keys[j][pl.ds(at, width), :], NT)
        dp = dot(gs[:rows], keys[j][pl.ds(KW + at, width), :], NT)
        return s, dp

    def grads(j, at, width, rows, s, dp, allowed, old):
        wide = lambda col: jnp.concatenate([col[:rows]] * (width // HD), axis=1)
        p = jnp.exp2(s * C2 - wide(log_col))
        if allowed is not None:
            p = jnp.where(allowed, p, 0.0)
        ds = (p * (dp - wide(delta_col))).astype(BF16)
        p = p.astype(BF16)
        cols = pl.ds(at, width)
        for half, left, right in ((slice(0, HD), qt, ds), (slice(HD, 2 * HD), gt, p)):
            term = dot(left[:, :rows], right, NN)
            sums[j][half, cols] = term if old is None else old[half, cols] + term
        return dot(ds, keys[j][pl.ds(at, width), :], NN)

    dq[...] = jnp.zeros((rows_all, HD), F32) if dq_in is None else dq_in[...]
    part = 256
    steps = 2 if unit == "near" else 2 if nk == 2 else 1

    def step(n, carry):
        total = None
        chunks = [
            (j, at if steps == 1 else pl.multiple_of(n * (PK // steps) + at, part))
            for j in range(nk)
            for at in range(0, PK // steps, part)
        ]
        ahead = products(*chunks[0], part, rows_all)
        for m, (j, at) in enumerate(chunks):
            s, dp = ahead
            if m + 1 < len(chunks):
                ahead = products(*chunks[m + 1], part, rows_all)
            term = grads(j, at, part, rows_all, s, dp, None, sums_in[j])
            total = term if total is None else total + term
        dq[...] += total
        return carry

    if steps == 1:
        step(0, 0)
    else:
        lax.fori_loop(0, steps, step, 0)

    if unit != "opp":
        y, xh, c = place[0], place[1], place[2]
        qi = 4 * (y if unit == "own" else (y + 1) % 4) + 2 * xh + c
        for j, (other_chip, other_core) in enumerate(keys_of):
            kj = 4 * y + 2 * ((1 - xh) if other_chip else xh) + ((1 - c) if other_core else c)
            seen, end = kj <= qi, 0
            for r in range(lengths.shape[0]):
                end = end + lengths[r]
                seen = seen & ((end <= kj) | (end > qi))

            @pl.when(seen)
            def _():
                allowed = None
                if unit == "own":
                    row = lax.broadcasted_iota(jnp.int32, (QR, RK), 0)
                    key_at = lax.broadcasted_iota(jnp.int32, (QR, RK), 1)
                    token = (row // BLOCK) * SUB + row % SUB
                    allowed = (kj < qi) | (key_at <= token)
                s, dp = products(j, PK, RK, QR)
                dq[:QR, :] += grads(j, PK, RK, QR, s, dp, allowed, sums[j])

    if final:
        rounded = (dq[...] * SCALE).astype(BF16).reshape(-1, BLOCK, HD)
        if others:
            done[...] = rounded
            last = pltpu.make_async_copy(done, dq_out.at[(place[0] + 2) % 4], sems.at[2])
            last.start()
            for copy in copies + [last]:
                copy.wait()
        else:
            dq_out[...] = rounded.reshape(dq_out.shape)


def tiles(name, unit, place, lengths, pays, keys_of, keys, sums, dq=None, final=False, others=()):
    have_sums = tuple(g is not None for g in sums)
    operands = held(*pays, *keys)
    rows = QR * len(pays)
    aliases = {}
    for n, old in enumerate(list(sums) + [dq]):
        if old is not None:
            if not others and (n < len(keys) or not final):
                aliases[2 + len(operands)] = n
            operands += held(old)
    operands += held(*others)
    dq_shape = pltpu.VMEM((rows, HD), F32)
    if final:
        dq_shape = pltpu.VMEM((len(pays), SRC, BLOCK, HD) if unit == "near" else (SRC, BLOCK, HD), BF16)
    if others:
        dq_shape = pltpu.HBM((4, SRC, BLOCK, HD), BF16)
    shapes = [pltpu.VMEM((2 * HD, KW), F32)] * len(keys) + [dq_shape]
    *sums, dq = pl.pallas_call(
        functools.partial(tiles_kernel, (unit, tuple(keys_of), have_sums, dq is not None, final, len(others))),
        in_specs=[SSPEC] * 2 + [VSPEC] * len(operands),
        out_specs=[VSPEC] * len(keys) + [ANYSPEC if others else VSPEC],
        out_shape=shapes,
        scratch_shapes=[
            pltpu.VMEM((rows, HD), BF16),
            pltpu.VMEM((rows, HD), BF16),
            pltpu.VMEM((HD, rows), BF16),
            pltpu.VMEM((HD, rows), BF16),
            pltpu.VMEM((rows, HD), F32),
            pltpu.VMEM((rows, HD), F32),
            pltpu.VMEM((rows, HD) if final else (8, HD), F32),
            pltpu.VMEM((SRC, BLOCK, HD) if others else (1, 16, HD), BF16),
            pltpu.SemaphoreType.DMA((4,)),
        ],
        input_output_aliases=aliases,
        compiler_params=pltpu.CompilerParams(vmem_limit_bytes=(18 if unit == "near" else 12) << 20),
        cost_estimate=pl.CostEstimate(flops=1, bytes_accessed=1, transcendentals=0),
        name=name,
    )(place, lengths, *operands)
    return sums, dq


def finish_kernel(parts, out):
    for b in range(SRC):
        for h in range(GROUP):
            rows = slice(h * SUB, (h + 1) * SUB)
            terms = [parts[n * SRC + b, rows, :].astype(F32) for n in range(4)]
            col = (b * GROUP + h) * HD
            out[:, col : col + HD] = (terms[0] + terms[1] + terms[2] + terms[3]).astype(BF16)


def finish(parts):
    return pl.pallas_call(
        finish_kernel,
        in_specs=[VSPEC],
        out_specs=VSPEC,
        out_shape=jax.ShapeDtypeStruct((SUB, SRC * GROUP * HD), BF16),
        name="finish",
    )(*held(parts))


def close_kernel(own, core, chip_in, dk, dv, drk, drv, chip, sem):
    load = pltpu.make_async_copy(chip_in, chip, sem)
    load.start()
    load.wait()

    def total(rows, cols):
        part = own[rows, cols] + core[rows, cols] + chip[rows, cols].astype(F32)
        return part.T

    keys, values = slice(0, HD), slice(HD, 2 * HD)
    dk[...] = total(keys, slice(0, PK)) * SCALE
    drk[...] = total(keys, slice(PK, KW)) * SCALE
    dv[...] = total(values, slice(0, PK))
    drv[...] = total(values, slice(PK, KW))


def close(own, core, chip):
    shape = lambda rows: jax.ShapeDtypeStruct((rows, HD), F32)
    return pl.pallas_call(
        close_kernel,
        in_specs=[VSPEC, VSPEC, ANYSPEC],
        out_specs=[VSPEC] * 4,
        out_shape=[shape(PK), shape(PK), shape(RK), shape(RK)],
        scratch_shapes=[pltpu.VMEM((2 * HD, KW), BF16), pltpu.SemaphoreType.DMA],
        compiler_params=pltpu.CompilerParams(vmem_limit_bytes=16 << 20),
        name="close",
    )(*held(own, core), *in_hbm([chip]))


def shift(n, s):
    return [(i, (i + s) % n) for i in range(n)]


def after(values, *earlier):
    return lax.optimization_barrier((values, earlier))[0]


def shards(
    queries,
    out_grad,
    attn_out,
    log_totals,
    prompt_keys,
    prompt_values,
    rollout_keys,
    rollout_values,
    rollout_blocks,
):
    place = jnp.stack([lax.axis_index(Y), lax.axis_index(XH), lax.axis_index(C)])
    place = place.astype(jnp.int32)
    to_next, to_last, swap = shift(4, 1), shift(4, -1), shift(2, 1)

    logs = (log_totals * LOG2E).reshape(SRC, SUB, GROUP).transpose(0, 2, 1).reshape(SRC, 1, BLOCK)
    l1 = lax.reduce_precision(logs, 8, 7)
    l2 = lax.reduce_precision(logs - l1, 8, 7)
    logs = [p.astype(BF16) for p in (l1, l2, logs - l1 - l2)]
    logs = jnp.concatenate(logs + [jnp.zeros((SRC, PAY - LROW - 3, BLOCK), BF16)], axis=1)

    payload = pack(place, queries, out_grad, attn_out)
    own = lax.all_to_all(payload, BULK, split_axis=0, concat_axis=0, tiled=True)
    kv_own = join(*after((prompt_keys, rollout_keys, prompt_values, rollout_values), payload))
    kv_c = lax.ppermute(kv_own, C, swap)
    kv_x = lax.ppermute(after(kv_own, own), XH, swap)
    own = own.at[:, LROW:PAY, :].set(logs)
    up = lax.ppermute(own, Y, to_last)
    down = lax.ppermute(own, Y, to_next)

    def run(name, pays, keys_of, keys, sums, dq=None, final=False, others=()):
        unit = name.split("_")[0]
        return tiles(name, unit, place, rollout_blocks, pays, keys_of, keys, sums, dq, final, others)

    o_own, o_core, o_chip, o_both = (0, 0), (0, 1), (1, 0), (1, 1)
    here, far = [o_own, o_core], [o_chip, o_both]
    (g_own, g_c), dq_own = run("own_here", [own], here, [kv_own, kv_c], [None, None])
    kv_x = after(kv_x, dq_own)
    kv_xc = lax.ppermute(kv_x, C, swap)
    (g_x,), dq_own = run("own_chip", [own], [o_chip], [kv_x], [None], dq_own)
    up, down = after((up, down), dq_own)
    opp = lax.ppermute(after(own, up, down), Y, shift(4, 2))
    (g_xc,), dq_own = run("own_both", [own], [o_both], [kv_xc], [None], dq_own, True)
    near = after([up, down], dq_own)
    (g_x, g_xc), dq_near = run("near_far", near, far, [kv_x, kv_xc], [g_x, g_xc])
    (g_xc,), dq_opp = run("opp_both", [opp], [o_both], [kv_xc], [g_xc])
    from_core = lax.ppermute(g_xc, C, swap)
    (g_x,), dq_opp = run("opp_chip", [opp], [o_chip], [kv_x], [g_x], dq_opp)
    to_chip = (g_x + after(from_core, dq_opp)).astype(BF16)
    from_chip = lax.ppermute(to_chip, XH, swap)
    dq_near = after(dq_near, to_chip)
    (g_own, g_c), dq_near = run(
        "near_here", near, here, [kv_own, kv_c], [g_own, g_c], dq_near, True
    )
    (g_own, g_c), dq = run(
        "opp_here", [opp], here, [kv_own, kv_c], [g_own, g_c], dq_opp, True, [dq_own, dq_near]
    )
    from_c = lax.ppermute(g_c, C, swap)
    dq, from_chip = lax.optimization_barrier((dq, from_chip))
    dq = dq.reshape(4 * SRC, BLOCK, HD)
    parts = lax.all_to_all(dq, (Y,) + BULK, split_axis=0, concat_axis=0, tiled=True)
    dk, dv, drk, drv = close(g_own, from_c, from_chip)
    query_grad = finish(after(parts, dk))
    return (query_grad, dk, dv, drk, drv)


def solution(mesh):
    fine = Mesh(mesh.devices.reshape(4, 2, 2, 4, 2), (Y, XH, C, Z, XL))
    hold, bulk = (Y, XH, C), (Z, XL)
    tokens = P(hold + bulk, None)
    split = P(hold, bulk)
    return jax.shard_map(
        shards,
        mesh=fine,
        in_specs=(tokens, tokens, tokens, split, split, split, split, split, P()),
        out_specs=(tokens, split, split, split, split),
        check_vma=False,
    )
```

```python
import functools

import jax
import jax.numpy as jnp
from jax import lax
from jax.experimental import pallas as pl
from jax.experimental.pallas import tpu as pltpu
from jax.sharding import Mesh
from jax.sharding import PartitionSpec as P

F32 = jnp.float32
BF16 = jnp.bfloat16
HD = 128
GROUP = 8
BLOCK = 128
NBLK = 16
PK = 1024
RK = 128
KW = PK + RK
QR = BLOCK * GROUP
SRC = 8
SUB = BLOCK // SRC
DROW = 2 * BLOCK
LROW = DROW + 8
PAY = LROW + 8
SCALE = HD ** (-0.5)
LOG2E = 1.4426950408889634
C2 = SCALE * LOG2E

NN = (((1,), (0,)), ((), ()))
NT = (((1,), (1,)), ((), ()))

Y, XH, C, Z, XL = "y", "xh", "c", "z", "xl"
BULK = (Z, XL)


def dot(a, b, dims):
    return lax.dot_general(a, b, dims, preferred_element_type=F32)


def held(*arrays):
    return [pltpu.with_memory_space_constraint(a, pltpu.VMEM) for a in arrays]


ANYSPEC = pl.BlockSpec(memory_space=pl.ANY)
VSPEC = pl.BlockSpec(memory_space=pltpu.VMEM)
SSPEC = pl.BlockSpec(memory_space=pltpu.SMEM)


def pieces_of(x):
    a = x.astype(BF16).astype(F32)
    b = (x - a).astype(BF16).astype(F32)
    return a, b, x - a - b


def pack_kernel(place, q_in, g_in, o_in, pay, q, g, o, sems):
    loads = [
        pltpu.make_async_copy(src, dst, sems.at[n])
        for n, (src, dst) in enumerate(((q_in, q), (g_in, g), (o_in, o)))
    ]
    for copy in loads:
        copy.start()
    for copy in loads:
        copy.wait()
    ones = jnp.ones((16, HD), BF16)
    row = lax.broadcasted_iota(jnp.int32, (16, BLOCK), 0)
    for b in range(SRC):
        prods = []
        for h in range(GROUP):
            cols = slice((b * GROUP + h) * HD, (b * GROUP + h + 1) * HD)
            qh, gh = q[:, cols], g[:, cols]
            pay[b, h * SUB : (h + 1) * SUB, :] = qh
            pay[b, BLOCK + h * SUB : BLOCK + (h + 1) * SUB, :] = gh
            prods.append(gh.astype(F32) * o[:, cols].astype(F32))
        prod = jnp.concatenate(prods, axis=0)
        high = prod.astype(BF16)
        low = (prod - high.astype(F32)).astype(BF16)
        d1, d2, d3 = pieces_of(dot(ones, high, NT) + dot(ones, low, NT))
        rows = jnp.where(row == 0, d1, jnp.where(row == 1, d2, jnp.where(row == 2, d3, 0.0)))
        pay[b, DROW:PAY, :] = rows.astype(BF16)


def in_hbm(arrays):
    return [pltpu.with_memory_space_constraint(a, pltpu.HBM) for a in arrays]


def pack(place, *arrays):
    return pl.pallas_call(
        pack_kernel,
        in_specs=[SSPEC] + [ANYSPEC] * 3,
        out_specs=VSPEC,
        out_shape=pltpu.VMEM((SRC, PAY, HD), BF16),
        scratch_shapes=[pltpu.VMEM((SUB, SRC * GROUP * HD), BF16)] * 3
        + [pltpu.SemaphoreType.DMA((3,))],
        compiler_params=pltpu.CompilerParams(vmem_limit_bytes=8 << 20),
        name="pack",
    )(place, *in_hbm(arrays))


def join_kernel(pk, rk, pv, rv, kv, sems):
    copies, at = [], 0
    for n, (src, rows) in enumerate(((pk, PK), (rk, RK), (pv, PK), (rv, RK))):
        copies.append(pltpu.make_async_copy(src, kv.at[pl.ds(at, rows)], sems.at[n]))
        at += rows
    for copy in copies:
        copy.start()
    for copy in copies:
        copy.wait()


def join(*arrays):
    return pl.pallas_call(
        join_kernel,
        in_specs=[ANYSPEC] * 4,
        out_specs=VSPEC,
        out_shape=pltpu.VMEM((2 * KW, HD), BF16),
        scratch_shapes=[pltpu.SemaphoreType.DMA((4,))],
        compiler_params=pltpu.CompilerParams(vmem_limit_bytes=4 << 20),
        name="join",
    )(*in_hbm(arrays))


def column(rows):
    line = jnp.concatenate([rows[s : s + 1, :] for s in range(SRC)], axis=1)
    return jnp.broadcast_to(line, (HD, QR)).T


def tiles_kernel(cfg, *refs):
    unit, keys_of, have_sums, have_dq, final, others = cfg
    nk = len(keys_of)
    refs = list(refs)

    def take(n):
        out = refs[:n]
        del refs[:n]
        return out

    place, lengths = take(2)
    pays = take(2 if unit == "near" else 1)
    rows_all = QR * len(pays)
    keys = take(nk)
    sums_in = [take(1)[0] if h else None for h in have_sums]
    dq_in = take(1)[0] if have_dq else None
    blocks = take(others)
    sums = take(nk)
    dq_out, qs, gs, qt, gt, log_col, delta_col, dqa, done, sems = refs
    dq = dqa if final else dq_out
    copies = []
    if blocks:
        parts = ((0, blocks[0]), (1, blocks[1].at[0]), (3, blocks[1].at[1]))
        for n, (back, block) in enumerate(parts):
            target = dq_out.at[(place[0] + back) % 4]
            copies.append(pltpu.make_async_copy(block, target, sems.at[n]))
    for copy in copies:
        copy.start()

    for m, pay in enumerate(pays):
        rows = slice(m * QR, (m + 1) * QR)
        qs[rows, :] = pay[:, 0:BLOCK, :].reshape(QR, HD)
        gs[rows, :] = pay[:, BLOCK : 2 * BLOCK, :].reshape(QR, HD)
        scalars = pay[:, DROW:PAY, :].astype(F32)
        add3 = lambda n: scalars[:, n, :] + scalars[:, n + 1, :] + scalars[:, n + 2, :]
        delta_col[rows, :] = column(add3(0))
        log_col[rows, :] = column(add3(LROW - DROW))
    qt[...] = qs[...].T
    gt[...] = gs[...].T
    for j in range(nk):
        tail = sums_in[j][:, PK:KW] if have_sums[j] else jnp.zeros((2 * HD, RK), F32)
        sums[j][:, PK:KW] = tail

    def products(j, at, width, rows):
        s = dot(qs[:rows], keys[j][pl.ds(at, width), :], NT)
        dp = dot(gs[:rows], keys[j][pl.ds(KW + at, width), :], NT)
        return s, dp

    def grads(j, at, width, rows, s, dp, allowed, old):
        wide = lambda col: jnp.concatenate([col[:rows]] * (width // HD), axis=1)
        p = jnp.exp2(s * C2 - wide(log_col))
        if allowed is not None:
            p = jnp.where(allowed, p, 0.0)
        ds = (p * (dp - wide(delta_col))).astype(BF16)
        p = p.astype(BF16)
        cols = pl.ds(at, width)
        for half, left, right in ((slice(0, HD), qt, ds), (slice(HD, 2 * HD), gt, p)):
            term = dot(left[:, :rows], right, NN)
            sums[j][half, cols] = term if old is None else old[half, cols] + term
        return dot(ds, keys[j][pl.ds(at, width), :], NN)

    dq[...] = jnp.zeros((rows_all, HD), F32) if dq_in is None else dq_in[...]
    part = 256
    steps = 2 if unit == "near" else 2 if nk == 2 else 1

    def step(n, carry):
        total = None
        chunks = [
            (j, at if steps == 1 else pl.multiple_of(n * (PK // steps) + at, part))
            for j in range(nk)
            for at in range(0, PK // steps, part)
        ]
        ahead = products(*chunks[0], part, rows_all)
        for m, (j, at) in enumerate(chunks):
            s, dp = ahead
            if m + 1 < len(chunks):
                ahead = products(*chunks[m + 1], part, rows_all)
            term = grads(j, at, part, rows_all, s, dp, None, sums_in[j])
            total = term if total is None else total + term
        dq[...] += total
        return carry

    if steps == 1:
        step(0, 0)
    else:
        lax.fori_loop(0, steps, step, 0)

    if unit != "opp":
        y, xh, c = place[0], place[1], place[2]
        qi = 4 * (y if unit == "own" else (y + 1) % 4) + 2 * xh + c
        for j, (other_chip, other_core) in enumerate(keys_of):
            kj = 4 * y + 2 * ((1 - xh) if other_chip else xh) + ((1 - c) if other_core else c)
            seen, end = kj <= qi, 0
            for r in range(lengths.shape[0]):
                end = end + lengths[r]
                seen = seen & ((end <= kj) | (end > qi))

            @pl.when(seen)
            def _():
                allowed = None
                if unit == "own":
                    row = lax.broadcasted_iota(jnp.int32, (QR, RK), 0)
                    key_at = lax.broadcasted_iota(jnp.int32, (QR, RK), 1)
                    token = (row // BLOCK) * SUB + row % SUB
                    allowed = (kj < qi) | (key_at <= token)
                s, dp = products(j, PK, RK, QR)
                dq[:QR, :] += grads(j, PK, RK, QR, s, dp, allowed, sums[j])

    if final:
        rounded = (dq[...] * SCALE).astype(BF16).reshape(-1, BLOCK, HD)
        if others:
            done[...] = rounded
            last = pltpu.make_async_copy(done, dq_out.at[(place[0] + 2) % 4], sems.at[2])
            last.start()
            for copy in copies + [last]:
                copy.wait()
        else:
            dq_out[...] = rounded.reshape(dq_out.shape)


def tiles(name, unit, place, lengths, pays, keys_of, keys, sums, dq=None, final=False, others=()):
    have_sums = tuple(g is not None for g in sums)
    operands = held(*pays, *keys)
    rows = QR * len(pays)
    aliases = {}
    for n, old in enumerate(list(sums) + [dq]):
        if old is not None:
            if not others and (n < len(keys) or not final):
                aliases[2 + len(operands)] = n
            operands += held(old)
    operands += held(*others)
    dq_shape = pltpu.VMEM((rows, HD), F32)
    if final:
        dq_shape = pltpu.VMEM((len(pays), SRC, BLOCK, HD) if unit == "near" else (SRC, BLOCK, HD), BF16)
    if others:
        dq_shape = pltpu.HBM((4, SRC, BLOCK, HD), BF16)
    shapes = [pltpu.VMEM((2 * HD, KW), F32)] * len(keys) + [dq_shape]
    *sums, dq = pl.pallas_call(
        functools.partial(tiles_kernel, (unit, tuple(keys_of), have_sums, dq is not None, final, len(others))),
        in_specs=[SSPEC] * 2 + [VSPEC] * len(operands),
        out_specs=[VSPEC] * len(keys) + [ANYSPEC if others else VSPEC],
        out_shape=shapes,
        scratch_shapes=[
            pltpu.VMEM((rows, HD), BF16),
            pltpu.VMEM((rows, HD), BF16),
            pltpu.VMEM((HD, rows), BF16),
            pltpu.VMEM((HD, rows), BF16),
            pltpu.VMEM((rows, HD), F32),
            pltpu.VMEM((rows, HD), F32),
            pltpu.VMEM((rows, HD) if final else (8, HD), F32),
            pltpu.VMEM((SRC, BLOCK, HD) if others else (1, 16, HD), BF16),
            pltpu.SemaphoreType.DMA((4,)),
        ],
        input_output_aliases=aliases,
        compiler_params=pltpu.CompilerParams(vmem_limit_bytes=(18 if unit == "near" else 12) << 20),
        cost_estimate=pl.CostEstimate(flops=1, bytes_accessed=1, transcendentals=0),
        name=name,
    )(place, lengths, *operands)
    return sums, dq


def finish_kernel(parts, out):
    for b in range(SRC):
        for h in range(GROUP):
            rows = slice(h * SUB, (h + 1) * SUB)
            terms = [parts[n * SRC + b, rows, :].astype(F32) for n in range(4)]
            col = (b * GROUP + h) * HD
            out[:, col : col + HD] = (terms[0] + terms[1] + terms[2] + terms[3]).astype(BF16)


def finish(parts):
    return pl.pallas_call(
        finish_kernel,
        in_specs=[VSPEC],
        out_specs=VSPEC,
        out_shape=jax.ShapeDtypeStruct((SUB, SRC * GROUP * HD), BF16),
        name="finish",
    )(*held(parts))


def close_kernel(own, core, chip_in, dk, dv, drk, drv, chip, sem):
    load = pltpu.make_async_copy(chip_in, chip, sem)
    load.start()
    load.wait()

    def total(rows, cols):
        part = own[rows, cols] + core[rows, cols] + chip[rows, cols].astype(F32)
        return part.T

    keys, values = slice(0, HD), slice(HD, 2 * HD)
    dk[...] = total(keys, slice(0, PK)) * SCALE
    drk[...] = total(keys, slice(PK, KW)) * SCALE
    dv[...] = total(values, slice(0, PK))
    drv[...] = total(values, slice(PK, KW))


def close(own, core, chip):
    shape = lambda rows: jax.ShapeDtypeStruct((rows, HD), F32)
    return pl.pallas_call(
        close_kernel,
        in_specs=[VSPEC, VSPEC, ANYSPEC],
        out_specs=[VSPEC] * 4,
        out_shape=[shape(PK), shape(PK), shape(RK), shape(RK)],
        scratch_shapes=[pltpu.VMEM((2 * HD, KW), BF16), pltpu.SemaphoreType.DMA],
        compiler_params=pltpu.CompilerParams(vmem_limit_bytes=16 << 20),
        name="close",
    )(*held(own, core), *in_hbm([chip]))


def shift(n, s):
    return [(i, (i + s) % n) for i in range(n)]


def after(values, *earlier):
    return lax.optimization_barrier((values, earlier))[0]


def shards(
    queries,
    out_grad,
    attn_out,
    log_totals,
    prompt_keys,
    prompt_values,
    rollout_keys,
    rollout_values,
    rollout_blocks,
):
    place = jnp.stack([lax.axis_index(Y), lax.axis_index(XH), lax.axis_index(C)])
    place = place.astype(jnp.int32)
    to_next, to_last, swap = shift(4, 1), shift(4, -1), shift(2, 1)

    logs = (log_totals * LOG2E).reshape(SRC, SUB, GROUP).transpose(0, 2, 1).reshape(SRC, 1, BLOCK)
    l1 = lax.reduce_precision(logs, 8, 7)
    l2 = lax.reduce_precision(logs - l1, 8, 7)
    logs = [p.astype(BF16) for p in (l1, l2, logs - l1 - l2)]
    logs = jnp.concatenate(logs + [jnp.zeros((SRC, PAY - LROW - 3, BLOCK), BF16)], axis=1)

    payload = pack(place, queries, out_grad, attn_out)
    own = lax.all_to_all(payload, BULK, split_axis=0, concat_axis=0, tiled=True)
    kv_own = join(*after((prompt_keys, rollout_keys, prompt_values, rollout_values), payload))
    kv_c = lax.ppermute(kv_own, C, swap)
    kv_x = lax.ppermute(kv_own, XH, swap)
    own = own.at[:, LROW:PAY, :].set(logs)
    up = lax.ppermute(own, Y, to_last)
    down = lax.ppermute(own, Y, to_next)

    def run(name, pays, keys_of, keys, sums, dq=None, final=False, others=()):
        unit = name.split("_")[0]
        return tiles(name, unit, place, rollout_blocks, pays, keys_of, keys, sums, dq, final, others)

    o_own, o_core, o_chip, o_both = (0, 0), (0, 1), (1, 0), (1, 1)
    here, far = [o_own, o_core], [o_chip, o_both]
    (g_own, g_c), dq_own = run("own_here", [own], here, [kv_own, kv_c], [None, None])
    kv_x = after(kv_x, dq_own)
    kv_xc = lax.ppermute(kv_x, C, swap)
    (g_x,), dq_own = run("own_chip", [own], [o_chip], [kv_x], [None], dq_own)
    up, down = after((up, down), dq_own)
    opp = lax.ppermute(after(own, up, down), Y, shift(4, 2))
    (g_xc,), dq_own = run("own_both", [own], [o_both], [kv_xc], [None], dq_own, True)
    near = after([up, down], dq_own)
    (g_x, g_xc), dq_near = run("near_far", near, far, [kv_x, kv_xc], [g_x, g_xc])
    (g_xc,), dq_opp = run("opp_both", [opp], [o_both], [kv_xc], [g_xc])
    from_core = lax.ppermute(g_xc, C, swap)
    (g_x,), dq_opp = run("opp_chip", [opp], [o_chip], [kv_x], [g_x], dq_opp)
    to_chip = (g_x + after(from_core, dq_opp)).astype(BF16)
    from_chip = lax.ppermute(to_chip, XH, swap)
    dq_near = after(dq_near, to_chip)
    (g_own, g_c), dq_near = run(
        "near_here", near, here, [kv_own, kv_c], [g_own, g_c], dq_near, True
    )
    (g_own, g_c), dq = run(
        "opp_here", [opp], here, [kv_own, kv_c], [g_own, g_c], dq_opp, True, [dq_own, dq_near]
    )
    from_c = lax.ppermute(g_c, C, swap)
    dq, from_chip = lax.optimization_barrier((dq, from_chip))
    dq = dq.reshape(4 * SRC, BLOCK, HD)
    parts = lax.all_to_all(dq, (Y,) + BULK, split_axis=0, concat_axis=0, tiled=True)
    dk, dv, drk, drv = close(g_own, from_c, from_chip)
    query_grad = finish(after(parts, dk))
    return (query_grad, dk, dv, drk, drv)


def solution(mesh):
    fine = Mesh(mesh.devices.reshape(4, 2, 2, 4, 2), (Y, XH, C, Z, XL))
    hold, bulk = (Y, XH, C), (Z, XL)
    tokens = P(hold + bulk, None)
    split = P(hold, bulk)
    return jax.shard_map(
        shards,
        mesh=fine,
        in_specs=(tokens, tokens, tokens, split, split, split, split, split, P()),
        out_specs=(tokens, split, split, split, split),
        check_vma=False,
    )
```

```python
import functools

import jax
import jax.numpy as jnp
from jax import lax
from jax.experimental import pallas as pl
from jax.experimental.pallas import tpu as pltpu
from jax.sharding import Mesh
from jax.sharding import PartitionSpec as P

F32 = jnp.float32
BF16 = jnp.bfloat16
HD = 128
GROUP = 8
BLOCK = 128
NBLK = 16
PK = 1024
RK = 128
KW = PK + RK
QR = BLOCK * GROUP
SRC = 8
SUB = BLOCK // SRC
DROW = 2 * BLOCK
LROW = DROW + 8
PAY = LROW + 8
SCALE = HD ** (-0.5)
LOG2E = 1.4426950408889634
C2 = SCALE * LOG2E

NN = (((1,), (0,)), ((), ()))
NT = (((1,), (1,)), ((), ()))

Y, XH, C, Z, XL = "y", "xh", "c", "z", "xl"
BULK = (Z, XL)


def dot(a, b, dims):
    return lax.dot_general(a, b, dims, preferred_element_type=F32)


def held(*arrays):
    return [pltpu.with_memory_space_constraint(a, pltpu.VMEM) for a in arrays]


ANYSPEC = pl.BlockSpec(memory_space=pl.ANY)
VSPEC = pl.BlockSpec(memory_space=pltpu.VMEM)
SSPEC = pl.BlockSpec(memory_space=pltpu.SMEM)


def pieces_of(x):
    a = x.astype(BF16).astype(F32)
    b = (x - a).astype(BF16).astype(F32)
    return a, b, x - a - b


def pack_kernel(place, q_in, g_in, o_in, pay, q, g, o, sems):
    loads = [
        pltpu.make_async_copy(src, dst, sems.at[n])
        for n, (src, dst) in enumerate(((q_in, q), (g_in, g), (o_in, o)))
    ]
    for copy in loads:
        copy.start()
    for copy in loads:
        copy.wait()
    ones = jnp.ones((16, HD), BF16)
    row = lax.broadcasted_iota(jnp.int32, (16, BLOCK), 0)
    def destination(b, carry):
        prods = []
        for h in range(GROUP):
            cols = pl.ds(pl.multiple_of(b * GROUP * HD, GROUP * HD) + h * HD, HD)
            qh, gh = q[:, cols], g[:, cols]
            pay[b, h * SUB : (h + 1) * SUB, :] = qh
            pay[b, BLOCK + h * SUB : BLOCK + (h + 1) * SUB, :] = gh
            prods.append(gh.astype(F32) * o[:, cols].astype(F32))
        prod = jnp.concatenate(prods, axis=0)
        high = prod.astype(BF16)
        low = (prod - high.astype(F32)).astype(BF16)
        d1, d2, d3 = pieces_of(dot(ones, high, NT) + dot(ones, low, NT))
        rows = jnp.where(row == 0, d1, jnp.where(row == 1, d2, jnp.where(row == 2, d3, 0.0)))
        pay[b, DROW:PAY, :] = rows.astype(BF16)
        return carry

    lax.fori_loop(0, SRC, destination, 0)


def in_hbm(arrays):
    return [pltpu.with_memory_space_constraint(a, pltpu.HBM) for a in arrays]


def pack(place, *arrays):
    return pl.pallas_call(
        pack_kernel,
        in_specs=[SSPEC] + [ANYSPEC] * 3,
        out_specs=VSPEC,
        out_shape=pltpu.VMEM((SRC, PAY, HD), BF16),
        scratch_shapes=[pltpu.VMEM((SUB, SRC * GROUP * HD), BF16)] * 3
        + [pltpu.SemaphoreType.DMA((3,))],
        compiler_params=pltpu.CompilerParams(vmem_limit_bytes=8 << 20),
        name="pack",
    )(place, *in_hbm(arrays))


def join_kernel(pk, rk, pv, rv, kv, sems):
    copies, at = [], 0
    for n, (src, rows) in enumerate(((pk, PK), (rk, RK), (pv, PK), (rv, RK))):
        copies.append(pltpu.make_async_copy(src, kv.at[pl.ds(at, rows)], sems.at[n]))
        at += rows
    for copy in copies:
        copy.start()
    for copy in copies:
        copy.wait()


def join(*arrays):
    return pl.pallas_call(
        join_kernel,
        in_specs=[ANYSPEC] * 4,
        out_specs=VSPEC,
        out_shape=pltpu.VMEM((2 * KW, HD), BF16),
        scratch_shapes=[pltpu.SemaphoreType.DMA((4,))],
        compiler_params=pltpu.CompilerParams(vmem_limit_bytes=4 << 20),
        name="join",
    )(*in_hbm(arrays))


def column(rows):
    line = jnp.concatenate([rows[s : s + 1, :] for s in range(SRC)], axis=1)
    return jnp.broadcast_to(line, (HD, QR)).T


def tiles_kernel(cfg, *refs):
    unit, keys_of, have_sums, have_dq, final, others = cfg
    nk = len(keys_of)
    refs = list(refs)

    def take(n):
        out = refs[:n]
        del refs[:n]
        return out

    place, lengths = take(2)
    pays = take(2 if unit == "near" else 1)
    rows_all = QR * len(pays)
    keys = take(nk)
    sums_in = [take(1)[0] if h else None for h in have_sums]
    dq_in = take(1)[0] if have_dq else None
    blocks = take(others)
    sums = take(nk)
    dq_out, qs, gs, qt, gt, log_col, delta_col, dqa, done, sems = refs
    dq = dqa if final else dq_out
    copies = []
    if blocks:
        parts = ((0, blocks[0]), (1, blocks[1].at[0]), (3, blocks[1].at[1]))
        for n, (back, block) in enumerate(parts):
            target = dq_out.at[(place[0] + back) % 4]
            copies.append(pltpu.make_async_copy(block, target, sems.at[n]))
    for copy in copies:
        copy.start()

    for m, pay in enumerate(pays):
        rows = slice(m * QR, (m + 1) * QR)
        qs[rows, :] = pay[:, 0:BLOCK, :].reshape(QR, HD)
        gs[rows, :] = pay[:, BLOCK : 2 * BLOCK, :].reshape(QR, HD)
        scalars = pay[:, DROW:PAY, :].astype(F32)
        add3 = lambda n: scalars[:, n, :] + scalars[:, n + 1, :] + scalars[:, n + 2, :]
        delta_col[rows, :] = column(add3(0))
        log_col[rows, :] = column(add3(LROW - DROW))
    qt[...] = qs[...].T
    gt[...] = gs[...].T
    for j in range(nk):
        tail = sums_in[j][:, PK:KW] if have_sums[j] else jnp.zeros((2 * HD, RK), F32)
        sums[j][:, PK:KW] = tail

    def products(j, at, width, rows):
        s = dot(qs[:rows], keys[j][pl.ds(at, width), :], NT)
        dp = dot(gs[:rows], keys[j][pl.ds(KW + at, width), :], NT)
        return s, dp

    def grads(j, at, width, rows, s, dp, allowed, old):
        wide = lambda col: jnp.concatenate([col[:rows]] * (width // HD), axis=1)
        p = jnp.exp2(s * C2 - wide(log_col))
        if allowed is not None:
            p = jnp.where(allowed, p, 0.0)
        ds = (p * (dp - wide(delta_col))).astype(BF16)
        p = p.astype(BF16)
        cols = pl.ds(at, width)
        for half, left, right in ((slice(0, HD), qt, ds), (slice(HD, 2 * HD), gt, p)):
            term = dot(left[:, :rows], right, NN)
            sums[j][half, cols] = term if old is None else old[half, cols] + term
        return dot(ds, keys[j][pl.ds(at, width), :], NN)

    dq[...] = jnp.zeros((rows_all, HD), F32) if dq_in is None else dq_in[...]
    part = 256
    steps = 1 if nk == 1 or blocks else 2 if have_sums[0] or unit != "own" else 4

    def step(n, carry):
        total = None
        chunks = [
            (j, at if steps == 1 else pl.multiple_of(n * (PK // steps) + at, part))
            for j in range(nk)
            for at in range(0, PK // steps, part)
        ]
        ahead = products(*chunks[0], part, rows_all)
        for m, (j, at) in enumerate(chunks):
            s, dp = ahead
            if m + 1 < len(chunks):
                ahead = products(*chunks[m + 1], part, rows_all)
            term = grads(j, at, part, rows_all, s, dp, None, sums_in[j])
            total = term if total is None else total + term
        dq[...] += total
        return carry

    if steps == 1:
        step(0, 0)
    else:
        lax.fori_loop(0, steps, step, 0)

    if unit != "opp":
        y, xh, c = place[0], place[1], place[2]
        qi = 4 * (y if unit == "own" else (y + 1) % 4) + 2 * xh + c
        for j, (other_chip, other_core) in enumerate(keys_of):
            kj = 4 * y + 2 * ((1 - xh) if other_chip else xh) + ((1 - c) if other_core else c)
            seen, end = kj <= qi, 0
            for r in range(lengths.shape[0]):
                end = end + lengths[r]
                seen = seen & ((end <= kj) | (end > qi))

            @pl.when(seen)
            def _():
                allowed = None
                if unit == "own" and not other_chip and not other_core:
                    row = lax.broadcasted_iota(jnp.int32, (QR, RK), 0)
                    key_at = lax.broadcasted_iota(jnp.int32, (QR, RK), 1)
                    token = (row // BLOCK) * SUB + row % SUB
                    allowed = key_at <= token
                s, dp = products(j, PK, RK, QR)
                dq[:QR, :] += grads(j, PK, RK, QR, s, dp, allowed, sums[j])

    if final:
        rounded = (dq[...] * SCALE).astype(BF16).reshape(-1, BLOCK, HD)
        if others:
            done[...] = rounded
            last = pltpu.make_async_copy(done, dq_out.at[(place[0] + 2) % 4], sems.at[2])
            last.start()
            for copy in copies + [last]:
                copy.wait()
        else:
            dq_out[...] = rounded.reshape(dq_out.shape)


def tiles(name, unit, place, lengths, pays, keys_of, keys, sums, dq=None, final=False, others=()):
    have_sums = tuple(g is not None for g in sums)
    operands = held(*pays, *keys)
    rows = QR * len(pays)
    aliases = {}
    for n, old in enumerate(list(sums) + [dq]):
        if old is not None:
            if not others and (n < len(keys) or not final):
                aliases[2 + len(operands)] = n
            operands += held(old)
    operands += held(*others)
    dq_shape = pltpu.VMEM((rows, HD), F32)
    if final:
        dq_shape = pltpu.VMEM((len(pays), SRC, BLOCK, HD) if unit == "near" else (SRC, BLOCK, HD), BF16)
    if others:
        dq_shape = pltpu.HBM((4, SRC, BLOCK, HD), BF16)
    shapes = [pltpu.VMEM((2 * HD, KW), F32)] * len(keys) + [dq_shape]
    *sums, dq = pl.pallas_call(
        functools.partial(tiles_kernel, (unit, tuple(keys_of), have_sums, dq is not None, final, len(others))),
        in_specs=[SSPEC] * 2 + [VSPEC] * len(operands),
        out_specs=[VSPEC] * len(keys) + [ANYSPEC if others else VSPEC],
        out_shape=shapes,
        scratch_shapes=[
            pltpu.VMEM((rows, HD), BF16),
            pltpu.VMEM((rows, HD), BF16),
            pltpu.VMEM((HD, rows), BF16),
            pltpu.VMEM((HD, rows), BF16),
            pltpu.VMEM((rows, HD), F32),
            pltpu.VMEM((rows, HD), F32),
            pltpu.VMEM((rows, HD) if final else (8, HD), F32),
            pltpu.VMEM((SRC, BLOCK, HD) if others else (1, 16, HD), BF16),
            pltpu.SemaphoreType.DMA((4,)),
        ],
        input_output_aliases=aliases,
        compiler_params=pltpu.CompilerParams(vmem_limit_bytes=(18 if unit == "near" else 12) << 20),
        cost_estimate=pl.CostEstimate(flops=1, bytes_accessed=1, transcendentals=0),
        name=name,
    )(place, lengths, *operands)
    return sums, dq


def finish_kernel(parts, out):
    def group(b, carry):
        at = pl.multiple_of(b * GROUP * HD, GROUP * HD)
        for h in range(GROUP):
            rows = slice(h * SUB, (h + 1) * SUB)
            terms = [parts[n * SRC + b, rows, :].astype(F32) for n in range(4)]
            total = terms[0] + terms[1] + terms[2] + terms[3]
            out[:, pl.ds(at + h * HD, HD)] = total.astype(BF16)
        return carry

    lax.fori_loop(0, SRC, group, 0)


def finish(parts):
    return pl.pallas_call(
        finish_kernel,
        in_specs=[VSPEC],
        out_specs=VSPEC,
        out_shape=jax.ShapeDtypeStruct((SUB, SRC * GROUP * HD), BF16),
        name="finish",
    )(*held(parts))


def close_kernel(own, core, chip_in, dk, dv, drk, drv, chip, sem):
    load = pltpu.make_async_copy(chip_in, chip, sem)
    load.start()
    load.wait()

    def total(rows, cols):
        part = own[rows, cols] + core[rows, cols] + chip[rows, cols].astype(F32)
        return part.T

    keys, values = slice(0, HD), slice(HD, 2 * HD)
    dk[...] = total(keys, slice(0, PK)) * SCALE
    drk[...] = total(keys, slice(PK, KW)) * SCALE
    dv[...] = total(values, slice(0, PK))
    drv[...] = total(values, slice(PK, KW))


def close(own, core, chip):
    shape = lambda rows: jax.ShapeDtypeStruct((rows, HD), F32)
    return pl.pallas_call(
        close_kernel,
        in_specs=[VSPEC, VSPEC, ANYSPEC],
        out_specs=[VSPEC] * 4,
        out_shape=[shape(PK), shape(PK), shape(RK), shape(RK)],
        scratch_shapes=[pltpu.VMEM((2 * HD, KW), BF16), pltpu.SemaphoreType.DMA],
        compiler_params=pltpu.CompilerParams(vmem_limit_bytes=16 << 20),
        name="close",
    )(*held(own, core), *in_hbm([chip]))


def shift(n, s):
    return [(i, (i + s) % n) for i in range(n)]


def after(values, *earlier):
    return lax.optimization_barrier((values, earlier))[0]


def shards(
    queries,
    out_grad,
    attn_out,
    log_totals,
    prompt_keys,
    prompt_values,
    rollout_keys,
    rollout_values,
    rollout_blocks,
):
    place = jnp.stack([lax.axis_index(Y), lax.axis_index(XH), lax.axis_index(C)])
    place = place.astype(jnp.int32)
    to_next, to_last, swap = shift(4, 1), shift(4, -1), shift(2, 1)

    logs = (log_totals * LOG2E).reshape(SRC, SUB, GROUP).transpose(0, 2, 1).reshape(SRC, 1, BLOCK)
    l1 = lax.reduce_precision(logs, 8, 7)
    l2 = lax.reduce_precision(logs - l1, 8, 7)
    logs = [p.astype(BF16) for p in (l1, l2, logs - l1 - l2)]
    logs = jnp.concatenate(logs + [jnp.zeros((SRC, PAY - LROW - 3, BLOCK), BF16)], axis=1)

    payload = pack(place, queries, out_grad, attn_out)
    own = lax.all_to_all(payload, BULK, split_axis=0, concat_axis=0, tiled=True)
    kv_own = join(*after((prompt_keys, rollout_keys, prompt_values, rollout_values), payload))
    kv_c = lax.ppermute(kv_own, C, swap)
    kv_x = lax.ppermute(kv_own, XH, swap)
    own = own.at[:, LROW:PAY, :].set(logs)
    up = lax.ppermute(own, Y, to_last)
    down = lax.ppermute(own, Y, to_next)

    def run(name, pays, keys_of, keys, sums, dq=None, final=False, others=()):
        unit = name.split("_")[0]
        return tiles(name, unit, place, rollout_blocks, pays, keys_of, keys, sums, dq, final, others)

    o_own, o_core, o_chip, o_both = (0, 0), (0, 1), (1, 0), (1, 1)
    here, far = [o_own, o_core], [o_chip, o_both]
    (g_own, g_c), dq_own = run("own_here", [own], here, [kv_own, kv_c], [None, None])
    kv_x = after(kv_x, dq_own)
    kv_xc = lax.ppermute(kv_x, C, swap)
    (g_x,), dq_own = run("own_chip", [own], [o_chip], [kv_x], [None], dq_own)
    up, down = after((up, down), dq_own)
    opp = lax.ppermute(after(own, up, down), Y, shift(4, 2))
    (g_xc,), dq_own = run("own_both", [own], [o_both], [kv_xc], [None], dq_own, True)
    near = after([up, down], dq_own)
    (g_x, g_xc), dq_near = run("near_far", near, far, [kv_x, kv_xc], [g_x, g_xc])
    (g_xc,), dq_opp = run("opp_both", [opp], [o_both], [kv_xc], [g_xc])
    from_core = lax.ppermute(g_xc, C, swap)
    (g_x,), dq_opp = run("opp_chip", [opp], [o_chip], [kv_x], [g_x], dq_opp)
    to_chip = (g_x + after(from_core, dq_opp)).astype(BF16)
    from_chip = lax.ppermute(to_chip, XH, swap)
    dq_near = after(dq_near, to_chip)
    (g_own, g_c), dq_near = run(
        "near_here", near, here, [kv_own, kv_c], [g_own, g_c], dq_near, True
    )
    (g_own, g_c), dq = run(
        "opp_here", [opp], here, [kv_own, kv_c], [g_own, g_c], dq_opp, True, [dq_own, dq_near]
    )
    from_c = lax.ppermute(g_c, C, swap)
    dq, from_chip = lax.optimization_barrier((dq, from_chip))
    dq = dq.reshape(4 * SRC, BLOCK, HD)
    parts = lax.all_to_all(dq, (Y,) + BULK, split_axis=0, concat_axis=0, tiled=True)
    dk, dv, drk, drv = close(g_own, from_c, from_chip)
    query_grad = finish(after(parts, dk))
    return (query_grad, dk, dv, drk, drv)


def solution(mesh):
    fine = Mesh(mesh.devices.reshape(4, 2, 2, 4, 2), (Y, XH, C, Z, XL))
    hold, bulk = (Y, XH, C), (Z, XL)
    tokens = P(hold + bulk, None)
    split = P(hold, bulk)
    return jax.shard_map(
        shards,
        mesh=fine,
        in_specs=(tokens, tokens, tokens, split, split, split, split, split, P()),
        out_specs=(tokens, split, split, split, split),
        check_vma=False,
    )
```
